256 devices in a mesh: dp: 16 (over y, x), mp: 16 (over z, core).
Axes of the slice: x: 4, y: 4, z: 8, core: 2. Of those that a mesh axis runs over, the one named last changes fastest.
Arguments:
- tiles: bfloat16 [4096, 256, 256], P(('dp', 'mp')), may hold values from -0.046875 to 0.046875
- tile_rows: int32 [4096], P(('dp', 'mp')), may hold values from 0 to 3, as said below
- tile_cols: int32 [4096], P(('dp', 'mp')), may hold values from 0 to 7
- tile_count: int32 [256], P(('dp', 'mp')), may hold values from 5 to 16, as said below
- data_weight: float32 [16384], P('mp'), may hold values from 0.3 to 3
- depth_level: int32 [32768], P(('dp', 'mp')), may hold values from 0 to 31
- depth_reg: float32 [32], replicated, may hold values from 0.1 to 1
- right_side: float32 [32768, 128], P(('dp', 'mp')), may hold values from -6 to 6
Outputs:
- solution: float32 [32768, 128], P(('dp', 'mp'))
- residual: float32 [32768, 128], P(('dp', 'mp'))
The draws below stay inside these ranges and needn't reach their ends.
Inputs may be any that keep to these rules, and one draw needn't show every extreme that they name: Within one device's 16 slots the pairs (tile_rows, tile_cols) are distinct. `tile_count`: slots of a device at or beyond its count are padding; some device has all 16 slots live.
All inputs are finite; a program needn't handle non-finite values.
Results may differ from the reference program's by a relative error of at most 0.0072.
Values may be sent and summed in bfloat16 or wider, within the bound.
No kernel may reach another device: no remote copies, remote signals or barrier semaphores. Data moves between devices by JAX's collectives and lax.ppermute only.
A program may use at most 64 MiB of HBM per device.

```python
import math
import jax
import jax.numpy as jnp
from jax import lax

TILE = 256
PROBES = 128
ITERS = 2
LEVELS = 32
ROW_BLOCKS = 4
COL_BLOCKS = 8
TILES_DEV = 16
TILES = 4096
NDATA = 16384
NCELL = 32768
FAN_IN = 16384
N_MP = 16
DEVICES = 256


def tile_slots(key):
    keys = jax.random.split(key, DEVICES)
    orders = jax.vmap(lambda single: jax.random.permutation(single, ROW_BLOCKS * COL_BLOCKS))(keys)
    return orders[:, :TILES_DEV].reshape(-1).astype(jnp.int32)


def draw_tile_rows(key, part):
    slots = tile_slots(key)
    return (slots // COL_BLOCKS).astype(jnp.int32)


def draw_tile_cols(key, part):
    slots = tile_slots(key)
    return (slots % COL_BLOCKS).astype(jnp.int32)


def draw_tile_count(key, part):
    key = jax.random.fold_in(key, 5)
    lowest = max(1, TILES_DEV // 3)
    counts = jax.random.randint(key, (DEVICES,), lowest, TILES_DEV + 1, dtype=jnp.int32)
    chosen = jax.random.randint(jax.random.fold_in(key, 6), (), 0, DEVICES, dtype=jnp.int32)
    return jnp.where(jnp.arange(DEVICES, dtype=jnp.int32) == chosen, TILES_DEV, counts).astype(jnp.int32)


def set_ends(array, stream_key, least, largest):
    longest = array.shape.index(max(array.shape))
    spots = []
    for shift in (0, 1):
        where = [jax.random.randint(jax.random.fold_in(stream_key, axis), (), 0, length) for axis, length in enumerate(array.shape)]
        where[longest] = (where[longest] + shift) % array.shape[longest]
        spots.append(tuple(where))
    return array.at[spots[0]].set(least).at[spots[1]].set(largest)


def block_scale(key, shape, cuts, smallest, top_value):
    level, own = 1.0, jax.random.fold_in(key, 6)
    for dim, blocks in cuts:
        steps = jnp.exp(jax.random.uniform(jax.random.fold_in(own, dim), (blocks,), jnp.float32, smallest / len(cuts), top_value / len(cuts)))
        level = level * jnp.repeat(steps, shape[dim] // blocks).reshape([-1 if axis == dim else 1 for axis in range(len(shape))])
    return level


def normal_values(stream_key, shape, deviation, most, cuts=(), kind=jnp.bfloat16):
    result = jax.random.normal(stream_key, shape, jnp.float32) * deviation
    if len(cuts) > 0:
        result = block_scale(stream_key, shape, cuts, -0.22, 0.18) * result
    return jnp.clip(result, min=-most, max=most).astype(kind)


def setup_inputs(seed: int = 0) -> dict:
    seeds = jax.random.split(jax.random.key(seed), 9)
    return {
        "tiles": normal_values(seeds[0], (TILES, TILE, TILE), FAN_IN ** -0.5, 0.046875, ((0, 256),)),
        "tile_rows": draw_tile_rows(jax.random.fold_in(seeds[8], 71), 0),
        "tile_cols": draw_tile_cols(jax.random.fold_in(seeds[8], 71), 0),
        "tile_count": draw_tile_count(jax.random.fold_in(seeds[8], 71), 0),
        "data_weight": jnp.clip(jnp.exp(math.log(3.0) - 2.3025851 * jax.random.uniform(seeds[4], (NDATA,), jnp.float32) ** block_scale(seeds[4], (NDATA,), ((0, 16),), -0.2, 0.2)), 0.3, 3.0),
        "depth_level": set_ends(jax.random.randint(seeds[5], (NCELL,), 0, LEVELS), jax.random.fold_in(seeds[5], 1), 0, LEVELS - 1).astype(jnp.int32),
        "depth_reg": jnp.clip(jnp.exp(jax.random.uniform(seeds[6], (LEVELS,), jnp.float32, math.log(0.1), math.log(1.0))), 0.1, 1.0),
        "right_side": normal_values(seeds[7], (NCELL, PROBES), 1.0, 6.0, ((0, 256),), jnp.float32),
    }


def reference(tiles, tile_rows, tile_cols, tile_count, data_weight, depth_level, depth_reg, right_side):
    slots = TILES_DEV
    reg_cell = depth_reg[depth_level]
    high = lax.Precision.HIGHEST
    positions = jnp.arange(slots, dtype=jnp.int32)

    def device_data(device):
        start = (device * slots).astype(jnp.int32)
        block = lax.dynamic_slice_in_dim(tiles, start, slots, 0).astype(jnp.float32)
        rows = lax.dynamic_slice_in_dim(tile_rows, start, slots, 0)
        cols = lax.dynamic_slice_in_dim(tile_cols, start, slots, 0)
        live = (positions < tile_count[device]).astype(jnp.float32)
        return block, rows, cols, live

    def forward(field):
        blocks = field.astype(jnp.bfloat16).reshape(NCELL // TILE, TILE, PROBES)

        def step(device, total):
            device = device.astype(jnp.int32)
            block, rows, cols, live = device_data(device)
            group_a = device // N_MP
            group_b = device % N_MP
            picked = blocks[(group_a * COL_BLOCKS + cols).astype(jnp.int32)].astype(jnp.float32)
            out = jnp.einsum("tab,tbr->tar", block, picked, precision=high)
            hot = (rows[None, :] == jnp.arange(ROW_BLOCKS, dtype=jnp.int32)[:, None]).astype(jnp.float32) * live[None, :]
            part = jnp.einsum("kt,tar->kar", hot, out, precision=high)
            base = (group_b * ROW_BLOCKS).astype(jnp.int32)
            current = lax.dynamic_slice_in_dim(total, base, ROW_BLOCKS, 0)
            return lax.dynamic_update_slice_in_dim(total, current + part, base, 0)

        total = lax.fori_loop(0, DEVICES, step, jnp.zeros((NDATA // TILE, TILE, PROBES), jnp.float32))
        return total.reshape(NDATA, PROBES)

    def backward(weighted):
        blocks = weighted.reshape(NDATA // TILE, TILE, PROBES)

        def step(device, total):
            device = device.astype(jnp.int32)
            block, rows, cols, live = device_data(device)
            group_a = device // N_MP
            group_b = device % N_MP
            picked = blocks[(group_b * ROW_BLOCKS + rows).astype(jnp.int32)].astype(jnp.float32)
            out = jnp.einsum("tab,tar->tbr", block, picked, precision=high)
            hot = (cols[None, :] == jnp.arange(COL_BLOCKS, dtype=jnp.int32)[:, None]).astype(jnp.float32) * live[None, :]
            part = jnp.einsum("kt,tar->kar", hot, out, precision=high)
            base = (group_a * COL_BLOCKS).astype(jnp.int32)
            current = lax.dynamic_slice_in_dim(total, base, COL_BLOCKS, 0)
            return lax.dynamic_update_slice_in_dim(total, current + part, base, 0)

        total = lax.fori_loop(0, DEVICES, step, jnp.zeros((NCELL // TILE, TILE, PROBES), jnp.float32))
        return total.reshape(NCELL, PROBES)

    def operate(field):
        predicted = forward(field)
        weighted = (data_weight[:, None] * predicted).astype(jnp.bfloat16)
        return backward(weighted) + reg_cell[:, None] * field

    solution = jnp.zeros_like(right_side)
    residual = right_side
    direction = right_side
    norm_now = jnp.sum(residual * residual, axis=0)
    for step_index in range(ITERS):
        image = operate(direction)
        alpha = norm_now / jnp.sum(direction * image, axis=0)
        solution = solution + alpha[None, :] * direction
        residual = residual - alpha[None, :] * image
        norm_next = jnp.sum(residual * residual, axis=0)
        direction = residual + (norm_next / norm_now)[None, :] * direction
        norm_now = norm_next
    return solution, residual
```

```python
import functools

import jax
import jax.numpy as jnp
from jax import lax
from jax.experimental import pallas as pl
from jax.experimental.pallas import tpu as pltpu
from jax.sharding import PartitionSpec as P

SUMS = 8
TERMS = 3
PARTS = 16
CORES = 2
SIDE = 4
KINDS = 3
COLS = 8
PACK = 2
TOP = 10.0
VMEM_LIMIT = 16 * 1024 * 1024


def call(kernel, out_shape, operands, smem=0, scratch=()):
    spaces = [pltpu.SMEM] * smem + [pltpu.VMEM] * (len(operands) - smem)
    return pl.pallas_call(
        kernel,
        out_shape=out_shape,
        in_specs=[pl.BlockSpec(memory_space=space) for space in spaces],
        out_specs=jax.tree.map(lambda _: pl.BlockSpec(memory_space=pltpu.VMEM), out_shape),
        scratch_shapes=list(scratch),
        compiler_params=pltpu.CompilerParams(vmem_limit_bytes=VMEM_LIMIT),
    )(*operands)


def f32(*shape):
    return jax.ShapeDtypeStruct(shape, jnp.float32)


def bf16(*shape):
    return jax.ShapeDtypeStruct(shape, jnp.bfloat16)


def rows_of(*sums):
    blank = jnp.zeros((SUMS - len(sums), sums[0].shape[1]), jnp.float32)
    return jnp.concatenate(list(sums) + [blank], axis=0)


def column_sum(value):
    return jnp.sum(value, axis=0, keepdims=True)


def cell_sums(value, reg, image):
    square = value * value
    return rows_of(column_sum(reg * square), column_sum(square), column_sum(value * image))


def start_kernel(right_ref, reg_ref, sums_ref):
    right = right_ref[...]
    sums_ref[...] = cell_sums(right, reg_ref[...], jnp.zeros_like(right))


def weight_column(part, weights):
    row = weights[pl.ds(part // PACK, 1), :]
    n = row.shape[1]
    shape = (n // PACK, n)
    wanted = lax.broadcasted_iota(jnp.int32, shape, 0) + lax.rem(part, PACK) * (n // PACK)
    same = lax.broadcasted_iota(jnp.int32, shape, 1) == wanted
    return jnp.sum(jnp.where(same, row, 0.0), axis=1, keepdims=True)


def split(sums):
    left, terms = sums, []
    for _ in range(TERMS):
        high = left.astype(jnp.bfloat16).astype(jnp.float32)
        terms.append(high)
        left = left - high
    return jnp.concatenate(terms, axis=0)


def join(terms):
    return terms[:KINDS] + terms[KINDS : 2 * KINDS] + terms[2 * KINDS : TERMS * KINDS]


def padded(rows):
    blank = jnp.zeros((PARTS - rows.shape[0], rows.shape[1]), jnp.float32)
    return jnp.concatenate([rows, blank], axis=0)


def exponent(largest):
    return jnp.ceil(jnp.log2(jnp.clip(largest, 1e-30, 1e30)))


def rows_at(start, size):
    return pl.ds(pl.multiple_of(start, size), size)


def row_of(slots, slot):
    return slots[slot] // COLS


def col_of(slots, slot):
    return lax.rem(slots[slot], COLS)


def forward_kernel(dp, slots, lower, upper, tiles, sums, out, total):
    tile = tiles.shape[1]
    chunk = out.shape[1]
    total[...] = jnp.zeros_like(total)
    for slot in range(tiles.shape[0]):
        col = col_of(slots, slot)
        source = jnp.concatenate([lower[col], upper[col]], axis=0)
        total[rows_at(row_of(slots, slot) * tile, tile), :] += jnp.dot(
            tiles[slot], source, preferred_element_type=jnp.float32
        )
    for part in range(out.shape[0]):
        out[part] = total[part * chunk : (part + 1) * chunk].astype(jnp.bfloat16)


def added(got):
    total = got[0].astype(jnp.float32)
    for part in range(1, got.shape[0]):
        total = total + got[part].astype(jnp.float32)
    return total


def weight_kernel(part, got, weights, sums, out):
    chunk = got.shape[1]
    predicted = added(got)
    weighted = (weight_column(part[0], weights) * predicted).astype(jnp.bfloat16)
    curve = column_sum(predicted * weighted.astype(jnp.float32)) + sums[0:1]
    extra = padded(split(jnp.concatenate([curve, sums[1:KINDS]], axis=0))).astype(jnp.bfloat16)
    for part in range(out.shape[0]):
        out[part, :chunk] = weighted
        out[part, chunk:] = extra


def backward(half, slots, got, tiles, source, total):
    tile = tiles.shape[1]
    parts, chunk = got.shape[0], got.shape[1] - PARTS
    cells = tile // CORES
    sums = got[0, chunk:].astype(jnp.float32)
    for part in range(1, parts):
        sums = sums + got[part, chunk:].astype(jnp.float32)
    for part in range(parts):
        source[part * chunk : (part + 1) * chunk] = got[part, :chunk]
    total[...] = jnp.zeros_like(total)
    for slot in range(tiles.shape[0]):
        total[rows_at(col_of(slots, slot) * cells, cells), :] += lax.dot_general(
            tiles[slot, :, rows_at(half * cells, cells)],
            source[rows_at(row_of(slots, slot) * tile, tile), :],
            (((0,), (0,)), ((), ())),
            preferred_element_type=jnp.float32,
        )
    return join(sums)


def backward_send_kernel(core, slots, got, tiles, coded, source, total):
    sums = backward(1 - core[0], slots, got, tiles, source, total)
    cells = tiles.shape[1] // CORES
    powers = []
    for block in range(total.shape[0] // cells):
        rows = slice(block * cells, (block + 1) * cells)
        power = exponent(jnp.max(jnp.abs(total[rows]), axis=0, keepdims=True))
        coded[rows] = total[rows] * jnp.exp2(TOP - power)
        powers.append(power)
    sum_power = exponent(jnp.abs(sums))
    terms = split(sums * jnp.exp2(TOP - sum_power))
    tail = padded(jnp.concatenate([terms, sum_power], axis=0))
    coded[total.shape[0] :] = jnp.concatenate([tail] + powers, axis=0)


def backward_keep_kernel(core, slots, got, tiles, after, keep, sums_out, source):
    sums = backward(core[0], slots, got, tiles, source, keep)
    sums_out[...] = rows_of(*[sums[kind : kind + 1] for kind in range(KINDS)])


def pair_kernel(keep, kept_sums, coded, out):
    blocks = out.shape[0]
    cells = out.shape[1] - PARTS
    tail = coded[blocks * cells :]
    at = TERMS * KINDS
    sums = kept_sums[:KINDS] + join(tail[:at]) * jnp.exp2(tail[at : at + KINDS] - TOP)
    sum_power = exponent(jnp.abs(sums))
    sums = split(sums * jnp.exp2(TOP - sum_power))
    for block in range(blocks):
        rows = slice(block * cells, (block + 1) * cells)
        back = jnp.exp2(tail[PARTS + block : PARTS + block + 1] - TOP)
        total = keep[rows] + coded[rows] * back
        power = exponent(jnp.max(jnp.abs(total), axis=0, keepdims=True))
        out[block, :cells] = total * jnp.exp2(TOP - power)
        out[block, cells:] = padded(jnp.concatenate([sums, sum_power, power], axis=0))


def summed(got, cells):
    total, sums = 0.0, 0.0
    at = cells + TERMS * KINDS
    for part in range(got.shape[0]):
        total = total + got[part, :cells] * jnp.exp2(got[part, at + KINDS : at + KINDS + 1] - TOP)
        sums = sums + join(got[part, cells:at]) * jnp.exp2(got[part, at : at + KINDS] - TOP)
    return total, sums


def first_update_kernel(got, right_ref, reg_ref, residual_ref, image_ref, low_ref, sums_ref, keep_ref):
    right, reg = right_ref[...], reg_ref[...]
    terms, sums = summed(got, right.shape[0])
    curve, norm = sums[0:1], sums[1:2]
    alpha = norm / curve
    image = terms + reg * right
    residual = right - alpha * image
    residual_ref[...] = residual
    image_ref[...] = image
    low = residual.astype(jnp.bfloat16)
    for block in range(low_ref.shape[0]):
        low_ref[block] = low
    sums_ref[...] = cell_sums(residual, reg, image)
    keep_ref[...] = rows_of(norm, curve, alpha)


def last_update_kernel(got, right_ref, reg_ref, residual_ref, image_ref, keep_ref, solution_out, residual_out):
    right, residual = right_ref[...], residual_ref[...]
    terms, sums = summed(got, right.shape[0])
    norm, curve, alpha = keep_ref[0:1], keep_ref[1:2], keep_ref[2:3]
    norm_next = sums[1:2]
    ratio = norm_next / norm
    image_next = terms + reg_ref[...] * residual + ratio * image_ref[...]
    curve_next = sums[0:1] + ratio * (2.0 * sums[2:3] + ratio * curve)
    alpha_next = norm_next / curve_next
    direction = residual + ratio * right
    solution_out[...] = alpha * right + alpha_next * direction
    residual_out[...] = residual - alpha_next * image_next


def exchange(value, axis):
    return lax.all_to_all(value, axis, 0, 0)


def swap(value):
    return lax.ppermute(value, "core", [(0, 1), (1, 0)])


def body(tiles, tile_rows, tile_cols, tile_count, data_weight, depth_level, depth_reg, right_side):
    tile = tiles.shape[1]
    cells, probes = right_side.shape
    group_rows = data_weight.shape[0]
    n_dp, n_z = lax.axis_size(DP), lax.axis_size("z")
    chunk = group_rows // n_dp
    col_blocks = cells * CORES * n_z // tile
    core = lax.axis_index("core").astype(jnp.int32).reshape(1)
    dp = lax.axis_index(DP).astype(jnp.int32).reshape(1)

    low = right_side.astype(jnp.bfloat16)
    own = exchange(jnp.broadcast_to(low, (n_z, cells, probes)), "z")
    own, tiles, tile_rows, tile_cols, tile_count, depth_level, depth_reg = lax.optimization_barrier(
        (own, tiles, tile_rows, tile_cols, tile_count, depth_level, depth_reg)
    )
    live = jnp.arange(tiles.shape[0], dtype=jnp.int32) < tile_count
    tiles = jnp.where(live[:, None, None], tiles, jnp.zeros_like(tiles))
    slots = tile_rows * COLS + tile_cols
    levels = jnp.arange(depth_reg.shape[0], dtype=jnp.int32)
    level_hot = (depth_level[:, None] == levels[None, :]).astype(jnp.float32)
    reg_cell = jnp.sum(level_hot * depth_reg[None, :], axis=1)
    reg = jnp.broadcast_to(reg_cell[:, None], (cells, probes))
    sums = call(start_kernel, f32(SUMS, probes), (right_side, reg))
    weights = data_weight.reshape(-1, chunk * PACK)

    def products(own, sums):
        other = swap(own)
        first = lax.axis_index("core") == 0
        lower, upper = jnp.where(first, own, other), jnp.where(first, other, own)
        partial = call(
            forward_kernel,
            bf16(n_dp, chunk, probes),
            (dp, slots, lower, upper, tiles, sums),
            smem=2,
            scratch=[pltpu.VMEM((group_rows, probes), jnp.float32)],
        )
        weighted = call(
            weight_kernel,
            bf16(n_dp, chunk + PARTS, probes),
            (dp, exchange(partial, DP), weights, sums),
            smem=1,
        )
        operands = (core, slots, exchange(weighted, DP), tiles)
        source = pltpu.VMEM((group_rows, probes), jnp.bfloat16)
        rows = n_z * cells
        coded = call(
            backward_send_kernel,
            f32(rows + PARTS + n_z, probes),
            operands,
            smem=2,
            scratch=[source, pltpu.VMEM((rows, probes), jnp.float32)],
        )
        keep, kept_sums = call(
            backward_keep_kernel,
            [f32(rows, probes), f32(SUMS, probes)],
            (*operands, coded),
            smem=2,
            scratch=[source],
        )
        coded = swap(coded.astype(jnp.float16)).astype(jnp.float32)
        terms = call(pair_kernel, f32(n_z, cells + PARTS, probes), (keep, kept_sums, coded))
        return exchange(terms.astype(jnp.float16), "z").astype(jnp.float32)

    whole, extra = f32(cells, probes), f32(SUMS, probes)
    residual, image, low, sums, keep = call(
        first_update_kernel,
        (whole, whole, bf16(n_z, cells, probes), extra, extra),
        (products(own, sums), right_side, reg),
    )
    return call(
        last_update_kernel,
        (whole, whole),
        (products(exchange(low, "z"), sums), right_side, reg, residual, image, keep),
    )


DP = ("y", "x")


def solution(mesh):
    n_dp, n_mp = mesh.devices.shape
    split_mesh = jax.sharding.Mesh(
        mesh.devices.reshape(n_dp // SIDE, SIDE, n_mp // CORES, CORES), ("y", "x", "z", "core")
    )
    mp = ("z", "core")
    every = DP + mp
    placed = (
        P(every, None, None),
        P(every),
        P(every),
        P(every),
        P(mp),
        P(every),
        P(),
        P(every, None),
    )
    return jax.shard_map(
        body,
        mesh=split_mesh,
        in_specs=placed,
        out_specs=(P(every, None), P(every, None)),
        check_vma=False,
    )
```

```python
import functools

import jax
import jax.numpy as jnp
from jax import lax
from jax.experimental import pallas as pl
from jax.experimental.pallas import tpu as pltpu
from jax.sharding import PartitionSpec as P

SUMS = 8
TERMS = 3
PARTS = 16
CORES = 2
SIDE = 4
KINDS = 3
COLS = 8
PACK = 2
TOP = 10.0
SUM_TOP = 14.0
VMEM_LIMIT = 16 * 1024 * 1024


def call(kernel, out_shape, operands, smem=0, scratch=()):
    spaces = [pltpu.SMEM] * smem + [pltpu.VMEM] * (len(operands) - smem)
    return pl.pallas_call(
        kernel,
        out_shape=out_shape,
        in_specs=[pl.BlockSpec(memory_space=space) for space in spaces],
        out_specs=jax.tree.map(lambda _: pl.BlockSpec(memory_space=pltpu.VMEM), out_shape),
        scratch_shapes=list(scratch),
        compiler_params=pltpu.CompilerParams(vmem_limit_bytes=VMEM_LIMIT),
    )(*operands)


def f32(*shape):
    return jax.ShapeDtypeStruct(shape, jnp.float32)


def bf16(*shape):
    return jax.ShapeDtypeStruct(shape, jnp.bfloat16)


def rows_of(*sums):
    blank = jnp.zeros((SUMS - len(sums), sums[0].shape[1]), jnp.float32)
    return jnp.concatenate(list(sums) + [blank], axis=0)


def column_sum(value):
    return jnp.sum(value, axis=0, keepdims=True)


def cell_sums(value, reg, image):
    square = value * value
    return rows_of(column_sum(reg * square), column_sum(square), column_sum(value * image))


def start_kernel(right_ref, reg_ref, sums_ref):
    right = right_ref[...]
    sums_ref[...] = cell_sums(right, reg_ref[...], jnp.zeros_like(right))


def weight_column(part, weights):
    row = weights[pl.ds(part // PACK, 1), :]
    n = row.shape[1]
    shape = (n // PACK, n)
    wanted = lax.broadcasted_iota(jnp.int32, shape, 0) + lax.rem(part, PACK) * (n // PACK)
    same = lax.broadcasted_iota(jnp.int32, shape, 1) == wanted
    return jnp.sum(jnp.where(same, row, 0.0), axis=1, keepdims=True)


def split(sums):
    left, terms = sums, []
    for _ in range(TERMS):
        high = left.astype(jnp.bfloat16).astype(jnp.float32)
        terms.append(high)
        left = left - high
    return jnp.concatenate(terms, axis=0)


def join(terms):
    return terms[:KINDS] + terms[KINDS : 2 * KINDS] + terms[2 * KINDS : TERMS * KINDS]


def padded(rows):
    blank = jnp.zeros((PARTS - rows.shape[0], rows.shape[1]), jnp.float32)
    return jnp.concatenate([rows, blank], axis=0)


def exponent(largest):
    return jnp.ceil(jnp.log2(jnp.clip(largest, 1e-30, 1e30)))


def rows_at(start, size):
    return pl.ds(pl.multiple_of(start, size), size)


def row_of(slots, slot):
    return slots[slot] // COLS


def col_of(slots, slot):
    return lax.rem(slots[slot], COLS)


def forward(half, slots, field, tiles, total):
    tile = tiles.shape[1]
    cells = tile // CORES
    for slot in range(tiles.shape[0]):
        total[rows_at(row_of(slots, slot) * tile, tile), :] += jnp.dot(
            tiles[slot, :, rows_at(half * cells, cells)],
            field[col_of(slots, slot)],
            preferred_element_type=jnp.float32,
        )


def forward_own_kernel(core, slots, own, tiles, total):
    total[...] = jnp.zeros_like(total)
    forward(core[0], slots, own, tiles, total)


def forward_other_kernel(dp, core, slots, other, tiles, own_total, sums, out, total):
    chunk = out.shape[1]
    total[...] = own_total[...]
    forward(1 - core[0], slots, other, tiles, total)
    for part in range(out.shape[0]):
        out[part] = total[part * chunk : (part + 1) * chunk].astype(jnp.bfloat16)


def added(got):
    total = got[0].astype(jnp.float32)
    for part in range(1, got.shape[0]):
        total = total + got[part].astype(jnp.float32)
    return total


def weight_kernel(part, got, weights, sums, out):
    chunk = got.shape[1]
    predicted = added(got)
    weighted = (weight_column(part[0], weights) * predicted).astype(jnp.bfloat16)
    curve = column_sum(predicted * weighted.astype(jnp.float32)) + sums[0:1]
    extra = padded(split(jnp.concatenate([curve, sums[1:KINDS]], axis=0))).astype(jnp.bfloat16)
    for part in range(out.shape[0]):
        out[part, :chunk] = weighted
        out[part, chunk:] = extra


def backward(half, slots, got, tiles, source, total):
    tile = tiles.shape[1]
    parts, chunk = got.shape[0], got.shape[1] - PARTS
    cells = tile // CORES
    sums = got[0, chunk:].astype(jnp.float32)
    for part in range(1, parts):
        sums = sums + got[part, chunk:].astype(jnp.float32)
    for part in range(parts):
        source[part * chunk : (part + 1) * chunk] = got[part, :chunk]
    total[...] = jnp.zeros_like(total)
    for slot in range(tiles.shape[0]):
        total[rows_at(col_of(slots, slot) * cells, cells), :] += lax.dot_general(
            tiles[slot, :, rows_at(half * cells, cells)],
            source[rows_at(row_of(slots, slot) * tile, tile), :],
            (((0,), (0,)), ((), ())),
            preferred_element_type=jnp.float32,
        )
    return join(sums)


def backward_send_kernel(core, slots, got, tiles, coded, source, total):
    sums = backward(1 - core[0], slots, got, tiles, source, total)
    cells = tiles.shape[1] // CORES
    powers = []
    for block in range(total.shape[0] // cells):
        rows = slice(block * cells, (block + 1) * cells)
        power = exponent(jnp.max(jnp.abs(total[rows]), axis=0, keepdims=True))
        coded[rows] = total[rows] * jnp.exp2(TOP - power)
        powers.append(power)
    sum_power = exponent(jnp.abs(sums))
    terms = split(sums * jnp.exp2(TOP - sum_power))
    tail = padded(jnp.concatenate([terms, sum_power], axis=0))
    coded[total.shape[0] :] = jnp.concatenate([tail] + powers, axis=0)


def backward_keep_kernel(core, slots, got, tiles, after, keep, sums_out, source):
    sums = backward(core[0], slots, got, tiles, source, keep)
    sums_out[...] = rows_of(*[sums[kind : kind + 1] for kind in range(KINDS)])


def pair_kernel(keep, kept_sums, coded, out):
    blocks = out.shape[0]
    cells = out.shape[1] - SUMS
    tail = coded[blocks * cells :]
    at = TERMS * KINDS
    sums = kept_sums[:KINDS] + join(tail[:at]) * jnp.exp2(tail[at : at + KINDS] - TOP)
    sum_power = exponent(jnp.max(jnp.abs(sums), axis=0, keepdims=True))
    sums = sums * jnp.exp2(SUM_TOP - sum_power)
    high = sums.astype(jnp.bfloat16).astype(jnp.float32)
    for block in range(blocks):
        rows = slice(block * cells, (block + 1) * cells)
        back = jnp.exp2(tail[PARTS + block : PARTS + block + 1] - TOP)
        total = keep[rows] + coded[rows] * back
        power = exponent(jnp.max(jnp.abs(total), axis=0, keepdims=True))
        out[block, :cells] = total * jnp.exp2(TOP - power)
        out[block, cells:] = jnp.concatenate([high, sums - high, sum_power, power], axis=0)


def summed(got, cells):
    total, sums = 0.0, 0.0
    for part in range(got.shape[0]):
        tail = got[part, cells:]
        total = total + got[part, :cells] * jnp.exp2(tail[2 * KINDS + 1 :] - TOP)
        high, low, power = tail[:KINDS], tail[KINDS : 2 * KINDS], tail[2 * KINDS : 2 * KINDS + 1]
        sums = sums + (high + low) * jnp.exp2(power - SUM_TOP)
    return total, sums


def first_update_kernel(got, right_ref, reg_ref, residual_ref, image_ref, low_ref, sums_ref, keep_ref):
    right, reg = right_ref[...], reg_ref[...]
    terms, sums = summed(got, right.shape[0])
    curve, norm = sums[0:1], sums[1:2]
    alpha = norm / curve
    image = terms + reg * right
    residual = right - alpha * image
    residual_ref[...] = residual
    image_ref[...] = image
    low = residual.astype(jnp.bfloat16)
    for block in range(low_ref.shape[0]):
        low_ref[block] = low
    sums_ref[...] = cell_sums(residual, reg, image)
    keep_ref[...] = rows_of(norm, curve, alpha)


def last_update_kernel(got, right_ref, reg_ref, residual_ref, image_ref, keep_ref, solution_out, residual_out):
    right, residual = right_ref[...], residual_ref[...]
    terms, sums = summed(got, right.shape[0])
    norm, curve, alpha = keep_ref[0:1], keep_ref[1:2], keep_ref[2:3]
    norm_next = sums[1:2]
    ratio = norm_next / norm
    image_next = terms + reg_ref[...] * residual + ratio * image_ref[...]
    curve_next = sums[0:1] + ratio * (2.0 * sums[2:3] + ratio * curve)
    alpha_next = norm_next / curve_next
    direction = residual + ratio * right
    solution_out[...] = alpha * right + alpha_next * direction
    residual_out[...] = residual - alpha_next * image_next


def exchange(value, axis):
    return lax.all_to_all(value, axis, 0, 0)


def swap(value):
    return lax.ppermute(value, "core", [(0, 1), (1, 0)])


def body(tiles, tile_rows, tile_cols, tile_count, data_weight, depth_level, depth_reg, right_side):
    tile = tiles.shape[1]
    cells, probes = right_side.shape
    group_rows = data_weight.shape[0]
    n_dp, n_z = lax.axis_size(DP), lax.axis_size("z")
    chunk = group_rows // n_dp
    col_blocks = cells * CORES * n_z // tile
    core = lax.axis_index("core").astype(jnp.int32).reshape(1)
    dp = lax.axis_index(DP).astype(jnp.int32).reshape(1)

    one = (jnp.arange(n_z, dtype=jnp.int32) + core >= 0).astype(jnp.float32)
    own = exchange((right_side[None] * one[:, None, None]).astype(jnp.bfloat16), "z")
    live = jnp.arange(tiles.shape[0], dtype=jnp.int32) < tile_count
    tiles = jnp.where(live[:, None, None], tiles, jnp.zeros_like(tiles))
    own = own * (tiles[0, :1, :1] == tiles[0, :1, :1]).astype(jnp.bfloat16)
    slots = tile_rows * COLS + tile_cols
    levels = jnp.arange(depth_reg.shape[0], dtype=jnp.int32)
    level_hot = (depth_level[:, None] == levels[None, :]).astype(jnp.float32)
    reg_cell = jnp.sum(level_hot * depth_reg[None, :], axis=1)
    reg = jnp.broadcast_to(reg_cell[:, None], (cells, probes))
    sums = call(start_kernel, f32(SUMS, probes), (right_side, reg))
    weights = data_weight.reshape(-1, chunk * PACK)

    def products(own, sums):
        total = call(
            forward_own_kernel, f32(group_rows, probes), (core, slots, own, tiles), smem=2
        )
        partial = call(
            forward_other_kernel,
            bf16(n_dp, chunk, probes),
            (dp, core, slots, swap(own), tiles, total, sums),
            smem=3,
            scratch=[pltpu.VMEM((group_rows, probes), jnp.float32)],
        )
        weighted = call(
            weight_kernel,
            bf16(n_dp, chunk + PARTS, probes),
            (dp, exchange(partial, DP), weights, sums),
            smem=1,
        )
        operands = (core, slots, exchange(weighted, DP), tiles)
        source = pltpu.VMEM((group_rows, probes), jnp.bfloat16)
        rows = n_z * cells
        coded = call(
            backward_send_kernel,
            f32(rows + PARTS + n_z, probes),
            operands,
            smem=2,
            scratch=[source, pltpu.VMEM((rows, probes), jnp.float32)],
        )
        keep, kept_sums = call(
            backward_keep_kernel,
            [f32(rows, probes), f32(SUMS, probes)],
            (*operands, coded),
            smem=2,
            scratch=[source],
        )
        coded = swap(coded.astype(jnp.float16)).astype(jnp.float32)
        terms = call(pair_kernel, f32(n_z, cells + SUMS, probes), (keep, kept_sums, coded))
        return exchange(terms.astype(jnp.float16), "z").astype(jnp.float32)

    whole, extra = f32(cells, probes), f32(SUMS, probes)
    residual, image, low, sums, keep = call(
        first_update_kernel,
        (whole, whole, bf16(n_z, cells, probes), extra, extra),
        (products(own, sums), right_side, reg),
    )
    return call(
        last_update_kernel,
        (whole, whole),
        (products(exchange(low, "z"), sums), right_side, reg, residual, image, keep),
    )


DP = ("y", "x")


def solution(mesh):
    n_dp, n_mp = mesh.devices.shape
    split_mesh = jax.sharding.Mesh(
        mesh.devices.reshape(n_dp // SIDE, SIDE, n_mp // CORES, CORES), ("y", "x", "z", "core")
    )
    mp = ("z", "core")
    every = DP + mp
    placed = (
        P(every, None, None),
        P(every),
        P(every),
        P(every),
        P(mp),
        P(every),
        P(),
        P(every, None),
    )
    return jax.shard_map(
        body,
        mesh=split_mesh,
        in_specs=placed,
        out_specs=(P(every, None), P(every, None)),
        check_vma=False,
    )
```

```python
import functools

import jax
import jax.numpy as jnp
from jax import lax
from jax.experimental import pallas as pl
from jax.experimental.pallas import tpu as pltpu
from jax.sharding import PartitionSpec as P

SUMS = 8
TERMS = 3
PARTS = 16
CORES = 2
SIDE = 4
KINDS = 3
COLS = 8
PACK = 2
TOP = 10.0
SUM_TOP = 14.0
VMEM_LIMIT = 16 * 1024 * 1024
VMEM_WHOLE = 60 * 1024 * 1024


def call(kernel, out_shape, operands, smem=0, scratch=()):
    spaces = [pltpu.SMEM] * smem + [pltpu.VMEM] * (len(operands) - smem)
    return pl.pallas_call(
        kernel,
        out_shape=out_shape,
        in_specs=[pl.BlockSpec(memory_space=space) for space in spaces],
        out_specs=jax.tree.map(lambda _: pl.BlockSpec(memory_space=pltpu.VMEM), out_shape),
        scratch_shapes=list(scratch),
        compiler_params=pltpu.CompilerParams(vmem_limit_bytes=VMEM_LIMIT),
    )(*operands)


def f32(*shape):
    return jax.ShapeDtypeStruct(shape, jnp.float32)


def bf16(*shape):
    return jax.ShapeDtypeStruct(shape, jnp.bfloat16)


def rows_of(*sums):
    blank = jnp.zeros((SUMS - len(sums), sums[0].shape[1]), jnp.float32)
    return jnp.concatenate(list(sums) + [blank], axis=0)


def column_sum(value):
    return jnp.sum(value, axis=0, keepdims=True)


def cell_sums(value, reg, image):
    square = value * value
    return rows_of(column_sum(reg * square), column_sum(square), column_sum(value * image))


def copies_kernel(right_in, low_out, right, low, sems):
    load = pltpu.make_async_copy(right_in, right, sems.at[0])
    load.start()
    load.wait()
    low[...] = right[...].astype(jnp.bfloat16)
    stores = [
        pltpu.make_async_copy(low, low_out.at[block], sems.at[block + 1])
        for block in range(low_out.shape[0])
    ]
    for store in stores:
        store.start()
    for store in stores:
        store.wait()


def start_kernel(right_ref, reg_ref, sums_ref):
    right = right_ref[...]
    sums_ref[...] = cell_sums(right, reg_ref[...], jnp.zeros_like(right))


def weight_column(part, weights):
    row = weights[pl.ds(part // PACK, 1), :]
    n = row.shape[1]
    shape = (n // PACK, n)
    wanted = lax.broadcasted_iota(jnp.int32, shape, 0) + lax.rem(part, PACK) * (n // PACK)
    same = lax.broadcasted_iota(jnp.int32, shape, 1) == wanted
    return jnp.sum(jnp.where(same, row, 0.0), axis=1, keepdims=True)


def split(sums):
    left, terms = sums, []
    for _ in range(TERMS):
        high = left.astype(jnp.bfloat16).astype(jnp.float32)
        terms.append(high)
        left = left - high
    return jnp.concatenate(terms, axis=0)


def join(terms):
    return terms[:KINDS] + terms[KINDS : 2 * KINDS] + terms[2 * KINDS : TERMS * KINDS]


def padded(rows):
    blank = jnp.zeros((PARTS - rows.shape[0], rows.shape[1]), jnp.float32)
    return jnp.concatenate([rows, blank], axis=0)


def exponent(largest):
    return jnp.ceil(jnp.log2(jnp.clip(largest, 1e-30, 1e30)))


def rows_at(start, size):
    return pl.ds(pl.multiple_of(start, size), size)


def row_of(slots, slot):
    return slots[slot] // COLS


def col_of(slots, slot):
    return lax.rem(slots[slot], COLS)


def forward(half, slots, field, tiles, total):
    tile = tiles.shape[1]
    cells = tile // CORES
    for slot in range(tiles.shape[0]):
        total[rows_at(row_of(slots, slot) * tile, tile), :] += jnp.dot(
            tiles[slot, :, rows_at(half * cells, cells)],
            field[col_of(slots, slot)],
            preferred_element_type=jnp.float32,
        )


def forward_own_kernel(core, slots, own, tiles, total):
    total[...] = jnp.zeros_like(total)
    forward(core[0], slots, own, tiles, total)


def forward_other_kernel(dp, core, slots, other, tiles, own_total, sums, out, total):
    chunk = out.shape[1]
    total[...] = own_total[...]
    forward(1 - core[0], slots, other, tiles, total)
    for part in range(out.shape[0]):
        out[part] = total[part * chunk : (part + 1) * chunk].astype(jnp.bfloat16)


def added(got):
    total = got[0].astype(jnp.float32)
    for part in range(1, got.shape[0]):
        total = total + got[part].astype(jnp.float32)
    return total


def weight_kernel(part, got, weights, sums, out):
    chunk = got.shape[1]
    predicted = added(got)
    weighted = (weight_column(part[0], weights) * predicted).astype(jnp.bfloat16)
    curve = column_sum(predicted * weighted.astype(jnp.float32)) + sums[0:1]
    extra = padded(split(jnp.concatenate([curve, sums[1:KINDS]], axis=0))).astype(jnp.bfloat16)
    for part in range(out.shape[0]):
        out[part, :chunk] = weighted
        out[part, chunk:] = extra


def backward(half, slots, got, tiles, source, total):
    tile = tiles.shape[1]
    parts, chunk = got.shape[0], got.shape[1] - PARTS
    cells = tile // CORES
    sums = got[0, chunk:].astype(jnp.float32)
    for part in range(1, parts):
        sums = sums + got[part, chunk:].astype(jnp.float32)
    for part in range(parts):
        source[part * chunk : (part + 1) * chunk] = got[part, :chunk]
    total[...] = jnp.zeros_like(total)
    for slot in range(tiles.shape[0]):
        total[rows_at(col_of(slots, slot) * cells, cells), :] += lax.dot_general(
            tiles[slot, :, rows_at(half * cells, cells)],
            source[rows_at(row_of(slots, slot) * tile, tile), :],
            (((0,), (0,)), ((), ())),
            preferred_element_type=jnp.float32,
        )
    return join(sums)


def backward_send_kernel(core, slots, got, tiles, coded, source, total):
    sums = backward(1 - core[0], slots, got, tiles, source, total)
    cells = tiles.shape[1] // CORES
    powers = []
    for block in range(total.shape[0] // cells):
        rows = slice(block * cells, (block + 1) * cells)
        power = exponent(jnp.max(jnp.abs(total[rows]), axis=0, keepdims=True))
        coded[rows] = total[rows] * jnp.exp2(TOP - power)
        powers.append(power)
    sum_power = exponent(jnp.abs(sums))
    terms = split(sums * jnp.exp2(TOP - sum_power))
    tail = padded(jnp.concatenate([terms, sum_power], axis=0))
    coded[total.shape[0] :] = jnp.concatenate([tail] + powers, axis=0)


def backward_keep_kernel(core, slots, got, tiles, after, keep, sums_out, source):
    sums = backward(core[0], slots, got, tiles, source, keep)
    sums_out[...] = rows_of(*[sums[kind : kind + 1] for kind in range(KINDS)])


def pair_kernel(keep, kept_sums, coded, out):
    blocks = out.shape[0]
    cells = out.shape[1] - SUMS
    tail = coded[blocks * cells :]
    at = TERMS * KINDS
    sums = kept_sums[:KINDS] + join(tail[:at]) * jnp.exp2(tail[at : at + KINDS] - TOP)
    sum_power = exponent(jnp.max(jnp.abs(sums), axis=0, keepdims=True))
    sums = sums * jnp.exp2(SUM_TOP - sum_power)
    high = sums.astype(jnp.bfloat16).astype(jnp.float32)
    for block in range(blocks):
        rows = slice(block * cells, (block + 1) * cells)
        back = jnp.exp2(tail[PARTS + block : PARTS + block + 1] - TOP)
        total = keep[rows] + coded[rows] * back
        power = exponent(jnp.max(jnp.abs(total), axis=0, keepdims=True))
        out[block, :cells] = total * jnp.exp2(TOP - power)
        out[block, cells:] = jnp.concatenate([high, sums - high, sum_power, power], axis=0)


def summed(got, cells):
    total, sums = 0.0, 0.0
    for part in range(got.shape[0]):
        tail = got[part, cells:]
        total = total + got[part, :cells] * jnp.exp2(tail[2 * KINDS + 1 :] - TOP)
        high, low, power = tail[:KINDS], tail[KINDS : 2 * KINDS], tail[2 * KINDS : 2 * KINDS + 1]
        sums = sums + (high + low) * jnp.exp2(power - SUM_TOP)
    return total, sums


def first_update_kernel(got, right_ref, reg_ref, residual_ref, image_ref, low_ref, sums_ref, keep_ref):
    right, reg = right_ref[...], reg_ref[...]
    terms, sums = summed(got, right.shape[0])
    curve, norm = sums[0:1], sums[1:2]
    alpha = norm / curve
    image = terms + reg * right
    residual = right - alpha * image
    residual_ref[...] = residual
    image_ref[...] = image
    low = residual.astype(jnp.bfloat16)
    for block in range(low_ref.shape[0]):
        low_ref[block] = low
    sums_ref[...] = cell_sums(residual, reg, image)
    keep_ref[...] = rows_of(norm, curve, alpha)


def last_update_kernel(got, right_ref, reg_ref, residual_ref, image_ref, keep_ref, solution_out, residual_out):
    right, residual = right_ref[...], residual_ref[...]
    terms, sums = summed(got, right.shape[0])
    norm, curve, alpha = keep_ref[0:1], keep_ref[1:2], keep_ref[2:3]
    norm_next = sums[1:2]
    ratio = norm_next / norm
    image_next = terms + reg_ref[...] * residual + ratio * image_ref[...]
    curve_next = sums[0:1] + ratio * (2.0 * sums[2:3] + ratio * curve)
    alpha_next = norm_next / curve_next
    direction = residual + ratio * right
    solution_out[...] = alpha * right + alpha_next * direction
    residual_out[...] = residual - alpha_next * image_next


def exchange(value, axis):
    return lax.all_to_all(value, axis, 0, 0)


def swap(value):
    return lax.ppermute(value, "core", [(0, 1), (1, 0)])


def body(tiles, tile_rows, tile_cols, tile_count, data_weight, depth_level, depth_reg, right_side):
    tile = tiles.shape[1]
    cells, probes = right_side.shape
    group_rows = data_weight.shape[0]
    n_dp, n_z = lax.axis_size(DP), lax.axis_size("z")
    chunk = group_rows // n_dp
    col_blocks = cells * CORES * n_z // tile
    core = lax.axis_index("core").astype(jnp.int32).reshape(1)
    dp = lax.axis_index(DP).astype(jnp.int32).reshape(1)

    anywhere = pl.BlockSpec(memory_space=pl.ANY)
    copies = pl.pallas_call(
        copies_kernel,
        out_shape=bf16(n_z, cells, probes),
        in_specs=[anywhere],
        out_specs=anywhere,
        scratch_shapes=[
            pltpu.VMEM((cells, probes), jnp.float32),
            pltpu.VMEM((cells, probes), jnp.bfloat16),
            pltpu.SemaphoreType.DMA((n_z + 1,)),
        ],
        compiler_params=pltpu.CompilerParams(vmem_limit_bytes=VMEM_WHOLE),
    )
    own = exchange(copies(right_side), "z")
    live = jnp.arange(tiles.shape[0], dtype=jnp.int32) < tile_count
    tiles = jnp.where(live[:, None, None], tiles, jnp.zeros_like(tiles))
    own = own * (tiles[0, :1, :1] == tiles[0, :1, :1]).astype(jnp.bfloat16)
    slots = tile_rows * COLS + tile_cols
    levels = jnp.arange(depth_reg.shape[0], dtype=jnp.int32)
    level_hot = (depth_level[:, None] == levels[None, :]).astype(jnp.float32)
    reg_cell = jnp.sum(level_hot * depth_reg[None, :], axis=1)
    reg = jnp.broadcast_to(reg_cell[:, None], (cells, probes))
    sums = call(start_kernel, f32(SUMS, probes), (right_side, reg))
    weights = data_weight.reshape(-1, chunk * PACK)

    def products(own, sums):
        total = call(
            forward_own_kernel, f32(group_rows, probes), (core, slots, own, tiles), smem=2
        )
        partial = call(
            forward_other_kernel,
            bf16(n_dp, chunk, probes),
            (dp, core, slots, swap(own), tiles, total, sums),
            smem=3,
            scratch=[pltpu.VMEM((group_rows, probes), jnp.float32)],
        )
        weighted = call(
            weight_kernel,
            bf16(n_dp, chunk + PARTS, probes),
            (dp, exchange(partial, DP), weights, sums),
            smem=1,
        )
        operands = (core, slots, exchange(weighted, DP), tiles)
        source = pltpu.VMEM((group_rows, probes), jnp.bfloat16)
        rows = n_z * cells
        coded = call(
            backward_send_kernel,
            f32(rows + PARTS + n_z, probes),
            operands,
            smem=2,
            scratch=[source, pltpu.VMEM((rows, probes), jnp.float32)],
        )
        keep, kept_sums = call(
            backward_keep_kernel,
            [f32(rows, probes), f32(SUMS, probes)],
            (*operands, coded),
            smem=2,
            scratch=[source],
        )
        coded = swap(coded.astype(jnp.float16)).astype(jnp.float32)
        terms = call(pair_kernel, f32(n_z, cells + SUMS, probes), (keep, kept_sums, coded))
        return exchange(terms.astype(jnp.float16), "z").astype(jnp.float32)

    whole, extra = f32(cells, probes), f32(SUMS, probes)
    residual, image, low, sums, keep = call(
        first_update_kernel,
        (whole, whole, bf16(n_z, cells, probes), extra, extra),
        (products(own, sums), right_side, reg),
    )
    return call(
        last_update_kernel,
        (whole, whole),
        (products(exchange(low, "z"), sums), right_side, reg, residual, image, keep),
    )


DP = ("y", "x")


def solution(mesh):
    n_dp, n_mp = mesh.devices.shape
    split_mesh = jax.sharding.Mesh(
        mesh.devices.reshape(n_dp // SIDE, SIDE, n_mp // CORES, CORES), ("y", "x", "z", "core")
    )
    mp = ("z", "core")
    every = DP + mp
    placed = (
        P(every, None, None),
        P(every),
        P(every),
        P(every),
        P(mp),
        P(every),
        P(),
        P(every, None),
    )
    return jax.shard_map(
        body,
        mesh=split_mesh,
        in_specs=placed,
        out_specs=(P(every, None), P(every, None)),
        check_vma=False,
    )
```

```python
import functools

import jax
import jax.numpy as jnp
from jax import lax
from jax.experimental import pallas as pl
from jax.experimental.pallas import tpu as pltpu
from jax.sharding import PartitionSpec as P

SUMS = 8
TERMS = 3
PARTS = 16
CORES = 2
SIDE = 4
KINDS = 3
CELLS = 128
FOUR = 4
COLS = 8
PACK = 2
TOP = 10.0
SUM_TOP = 14.0
VMEM_LIMIT = 16 * 1024 * 1024
VMEM_WHOLE = 60 * 1024 * 1024


def call(kernel, out_shape, operands, smem=0, scratch=()):
    spaces = [pltpu.SMEM] * smem + [pltpu.VMEM] * (len(operands) - smem)
    return pl.pallas_call(
        kernel,
        out_shape=out_shape,
        in_specs=[pl.BlockSpec(memory_space=space) for space in spaces],
        out_specs=jax.tree.map(lambda _: pl.BlockSpec(memory_space=pltpu.VMEM), out_shape),
        scratch_shapes=list(scratch),
        compiler_params=pltpu.CompilerParams(vmem_limit_bytes=VMEM_LIMIT),
    )(*operands)


def f32(*shape):
    return jax.ShapeDtypeStruct(shape, jnp.float32)


def bf16(*shape):
    return jax.ShapeDtypeStruct(shape, jnp.bfloat16)


def rows_of(*sums):
    blank = jnp.zeros((SUMS - len(sums), sums[0].shape[1]), jnp.float32)
    return jnp.concatenate(list(sums) + [blank], axis=0)


def column_sum(value):
    return jnp.sum(value, axis=0, keepdims=True)


def cell_sums(value, reg, image):
    square = value * value
    return rows_of(column_sum(reg * square), column_sum(square), column_sum(value * image))


def copies_kernel(right_in, low_out, right, low, sems):
    load = pltpu.make_async_copy(right_in, right, sems.at[0])
    load.start()
    load.wait()
    low[...] = right[...].astype(jnp.bfloat16)
    stores = [
        pltpu.make_async_copy(low, low_out.at[block], sems.at[block + 1])
        for block in range(low_out.shape[0])
    ]
    for store in stores:
        store.start()
    for store in stores:
        store.wait()


def start_kernel(right_ref, reg_ref, sums_ref):
    right = right_ref[...]
    sums_ref[...] = cell_sums(right, reg_ref[...], jnp.zeros_like(right))


def weight_column(part, weights):
    row = weights[pl.ds(part // PACK, 1), :]
    n = row.shape[1]
    shape = (n // PACK, n)
    wanted = lax.broadcasted_iota(jnp.int32, shape, 0) + lax.rem(part, PACK) * (n // PACK)
    same = lax.broadcasted_iota(jnp.int32, shape, 1) == wanted
    return jnp.sum(jnp.where(same, row, 0.0), axis=1, keepdims=True)


def split(sums):
    left, terms = sums, []
    for _ in range(TERMS):
        high = left.astype(jnp.bfloat16).astype(jnp.float32)
        terms.append(high)
        left = left - high
    return jnp.concatenate(terms, axis=0)


def join(terms):
    return terms[:KINDS] + terms[KINDS : 2 * KINDS] + terms[2 * KINDS : TERMS * KINDS]


def padded(rows):
    if rows.shape[0] == PARTS:
        return rows
    blank = jnp.zeros((PARTS - rows.shape[0], rows.shape[1]), jnp.float32)
    return jnp.concatenate([rows, blank], axis=0)


def exponent(largest):
    return jnp.ceil(jnp.log2(jnp.clip(largest, 1e-30, 1e30)))


def rows_at(start, size):
    return pl.ds(pl.multiple_of(start, size), size)


def row_of(slots, slot):
    return slots[slot] // COLS


def col_of(slots, slot):
    return lax.rem(slots[slot], COLS)


def forward(half, slots, field, tiles, total):
    tile = tiles.shape[1]
    cells = tile // CORES
    for slot in range(tiles.shape[0]):
        total[rows_at(row_of(slots, slot) * tile, tile), :] += jnp.dot(
            tiles[slot, :, rows_at(half * cells, cells)],
            field[col_of(slots, slot)],
            preferred_element_type=jnp.float32,
        )


def forward_own_kernel(core, slots, own, tiles, total):
    total[...] = jnp.zeros_like(total)
    forward(core[0], slots, own, tiles, total)


def forward_other_kernel(dp, core, slots, other, tiles, own_total, sums, out, total):
    chunk = out.shape[1]
    total[...] = own_total[...]
    forward(1 - core[0], slots, other, tiles, total)
    for part in range(out.shape[0]):
        out[part] = total[part * chunk : (part + 1) * chunk].astype(jnp.bfloat16)


def added(got):
    total = got[0].astype(jnp.float32)
    for part in range(1, got.shape[0]):
        total = total + got[part].astype(jnp.float32)
    return total


def weight_kernel(part, got, weights, sums, out):
    chunk = got.shape[1]
    predicted = added(got)
    weighted = (weight_column(part[0], weights) * predicted).astype(jnp.bfloat16)
    curve = column_sum(predicted * weighted.astype(jnp.float32)) + sums[0:1]
    extra = padded(split(jnp.concatenate([curve, sums[1:KINDS]], axis=0))).astype(jnp.bfloat16)
    for part in range(out.shape[0]):
        out[part, :chunk] = weighted
        out[part, chunk:] = extra


def backward(half, slots, got, tiles, source, total):
    tile = tiles.shape[1]
    parts, chunk = got.shape[0], got.shape[1] - PARTS
    cells = tile // CORES
    sums = got[0, chunk:].astype(jnp.float32)
    for part in range(1, parts):
        sums = sums + got[part, chunk:].astype(jnp.float32)
    for part in range(parts):
        source[part * chunk : (part + 1) * chunk] = got[part, :chunk]
    total[...] = jnp.zeros_like(total)
    for slot in range(tiles.shape[0]):
        total[rows_at(col_of(slots, slot) * cells, cells), :] += lax.dot_general(
            tiles[slot, :, rows_at(half * cells, cells)],
            source[rows_at(row_of(slots, slot) * tile, tile), :],
            (((0,), (0,)), ((), ())),
            preferred_element_type=jnp.float32,
        )
    return join(sums)


def backward_send_kernel(core, slots, got, tiles, coded, source, total):
    sums = backward(1 - core[0], slots, got, tiles, source, total)
    cells = tiles.shape[1] // CORES
    powers = []
    for block in range(total.shape[0] // cells):
        rows = slice(block * cells, (block + 1) * cells)
        power = exponent(jnp.max(jnp.abs(total[rows]), axis=0, keepdims=True))
        coded[rows] = total[rows] * jnp.exp2(TOP - power)
        powers.append(power)
    sum_power = exponent(jnp.abs(sums))
    terms = split(sums * jnp.exp2(TOP - sum_power))
    tail = padded(jnp.concatenate([terms, sum_power], axis=0))
    coded[total.shape[0] :] = jnp.concatenate([tail] + powers, axis=0)


def backward_keep_kernel(core, slots, got, tiles, after, keep, sums_out, source):
    sums = backward(core[0], slots, got, tiles, source, keep)
    sums_out[...] = rows_of(*[sums[kind : kind + 1] for kind in range(KINDS)])


def pair_kernel(keep, kept_sums, coded, out):
    blocks = out.shape[0]
    cells = out.shape[1] - SUMS
    tail = coded[blocks * cells :]
    at = TERMS * KINDS
    sums = kept_sums[:KINDS] + join(tail[:at]) * jnp.exp2(tail[at : at + KINDS] - TOP)
    sum_power = exponent(jnp.max(jnp.abs(sums), axis=0, keepdims=True))
    sums = sums * jnp.exp2(SUM_TOP - sum_power)
    high = sums.astype(jnp.bfloat16).astype(jnp.float32)
    for block in range(blocks):
        rows = slice(block * cells, (block + 1) * cells)
        back = jnp.exp2(tail[PARTS + block : PARTS + block + 1] - TOP)
        total = keep[rows] + coded[rows] * back
        power = exponent(jnp.max(jnp.abs(total), axis=0, keepdims=True))
        out[block, :cells] = total * jnp.exp2(TOP - power)
        out[block, cells:] = jnp.concatenate([high, sums - high, sum_power, power], axis=0)


def pair_sum(keep, kept_sums, coded, block):
    cells = CELLS
    blocks = keep.shape[0] // cells
    tail = coded[blocks * cells :]
    at = TERMS * KINDS
    sums = kept_sums[:KINDS] + join(tail[:at]) * jnp.exp2(tail[at : at + KINDS] - TOP)
    rows = slice(block * cells, (block + 1) * cells)
    back = jnp.exp2(tail[PARTS + block : PARTS + block + 1] - TOP)
    return keep[rows] + coded[rows] * back, sums


def emit(kept_blocks, sent_blocks, sums, kept, coded, kept_sums):
    cells = CELLS
    powers = []
    for at, block in enumerate(kept_blocks):
        kept[at * cells : (at + 1) * cells] = block
    for at, block in enumerate(sent_blocks):
        power = exponent(jnp.max(jnp.abs(block), axis=0, keepdims=True))
        coded[at * cells : (at + 1) * cells] = block * jnp.exp2(TOP - power)
        powers.append(power)
    power = exponent(jnp.abs(sums))
    terms = split(sums * jnp.exp2(TOP - power))
    coded[len(sent_blocks) * cells :] = padded(jnp.concatenate([terms, power] + powers, axis=0))
    kept_sums[...] = rows_of(*[sums[kind : kind + 1] for kind in range(KINDS)])


def absorb(kept, coded, kept_sums, order):
    cells = CELLS
    tail = coded[kept.shape[0] :]
    at = TERMS * KINDS
    blocks = []
    for block, place in enumerate(order):
        arrived = coded[place * cells : (place + 1) * cells]
        power = tail[at + KINDS + place : at + KINDS + place + 1]
        blocks.append(kept[block * cells : (block + 1) * cells] + arrived * jnp.exp2(power - TOP))
    return blocks, kept_sums[:KINDS] + join(tail[:at]) * jnp.exp2(tail[at : at + KINDS] - TOP)


def spread_kernel(height, keep, keep_sums, swapped, kept, coded, kept_sums, total):
    cells = CELLS
    for block in range(COLS):
        part, sums = pair_sum(keep, keep_sums, swapped, block)
        total[block * cells : (block + 1) * cells] = part
    half, own = height[0] // FOUR, lax.rem(height[0], FOUR)

    def blocks(chips):
        at = [z for chip in chips for z in (half * FOUR + chip, (2 - half) * FOUR - 1 - chip)]
        return [total[rows_at(z * cells, cells), :] for z in at]

    emit(
        blocks([own, jnp.bitwise_xor(own, 2)]),
        blocks([jnp.bitwise_xor(own, 1), jnp.bitwise_xor(own, 3)]),
        sums,
        kept,
        coded,
        kept_sums,
    )


def halve_kernel(kept_in, coded_in, sums_in, kept, coded, kept_sums):
    blocks, sums = absorb(kept_in, coded_in, sums_in, range(4))
    emit(blocks[:2], blocks[2:], sums, kept, coded, kept_sums)


def cross_kernel(kept_in, coded_in, sums_in, right_ref, reg_ref, kept, coded, kept_sums):
    (own, other), sums = absorb(kept_in, coded_in, sums_in, range(2))
    emit([own, other], [own + reg_ref[...] * right_ref[...], other], sums, kept, coded, kept_sums)


def summed(got, cells):
    total, sums = 0.0, 0.0
    for part in range(got.shape[0]):
        tail = got[part, cells:]
        total = total + got[part, :cells] * jnp.exp2(tail[2 * KINDS + 1 :] - TOP)
        high, low, power = tail[:KINDS], tail[KINDS : 2 * KINDS], tail[2 * KINDS : 2 * KINDS + 1]
        sums = sums + (high + low) * jnp.exp2(power - SUM_TOP)
    return total, sums


def first_update_kernel(
    height, kept, coded, kept_sums, gathered, right_ref, reg_ref, residual_ref, image_ref, low_ref, sums_ref, keep_ref
):
    (terms, other), sums = absorb(kept, coded, kept_sums, (1, 0))
    right, reg = right_ref[...], reg_ref[...]
    curve, norm = sums[0:1], sums[1:2]
    alpha = norm / curve
    image = terms + reg * right
    residual = right - alpha * image
    residual_ref[...] = residual
    image_ref[...] = image
    low_ref[0] = residual.astype(jnp.bfloat16)
    other_right = gathered[COLS - 1 - height[0]].astype(jnp.float32)
    low_ref[1] = (other_right - alpha * other).astype(jnp.bfloat16)
    sums_ref[...] = cell_sums(residual, reg, image)
    keep_ref[...] = rows_of(norm, curve, alpha)


def last_update_kernel(got, right_ref, reg_ref, residual_ref, image_ref, keep_ref, solution_out, residual_out):
    right, residual = right_ref[...], residual_ref[...]
    terms, sums = summed(got, right.shape[0])
    norm, curve, alpha = keep_ref[0:1], keep_ref[1:2], keep_ref[2:3]
    norm_next = sums[1:2]
    ratio = norm_next / norm
    image_next = terms + reg_ref[...] * residual + ratio * image_ref[...]
    curve_next = sums[0:1] + ratio * (2.0 * sums[2:3] + ratio * curve)
    alpha_next = norm_next / curve_next
    direction = residual + ratio * right
    solution_out[...] = alpha * right + alpha_next * direction
    residual_out[...] = residual - alpha_next * image_next


def exchange(value, axis):
    return lax.all_to_all(value, axis, 0, 0)


def along_z(value, to):
    pairs = [
        (z * CORES + core, to(z) * CORES + core)
        for z in range(lax.axis_size("z"))
        for core in range(CORES)
    ]
    return lax.ppermute(value, ("z", "core"), pairs)


def near(z):
    return z ^ 1


def far(z):
    return z ^ 2


def mirror(z):
    return COLS - 1 - z


def swap(value):
    return lax.ppermute(value, "core", [(0, 1), (1, 0)])


def body(tiles, tile_rows, tile_cols, tile_count, data_weight, depth_level, depth_reg, right_side):
    tile = tiles.shape[1]
    cells, probes = right_side.shape
    group_rows = data_weight.shape[0]
    n_dp, n_z = lax.axis_size(DP), lax.axis_size("z")
    chunk = group_rows // n_dp
    col_blocks = cells * CORES * n_z // tile
    core = lax.axis_index("core").astype(jnp.int32).reshape(1)
    height = lax.axis_index("z").astype(jnp.int32).reshape(1)
    dp = lax.axis_index(DP).astype(jnp.int32).reshape(1)

    anywhere = pl.BlockSpec(memory_space=pl.ANY)
    copies = pl.pallas_call(
        copies_kernel,
        out_shape=bf16(n_z, cells, probes),
        in_specs=[anywhere],
        out_specs=anywhere,
        scratch_shapes=[
            pltpu.VMEM((cells, probes), jnp.float32),
            pltpu.VMEM((cells, probes), jnp.bfloat16),
            pltpu.SemaphoreType.DMA((n_z + 1,)),
        ],
        compiler_params=pltpu.CompilerParams(vmem_limit_bytes=VMEM_WHOLE),
    )
    own = exchange(copies(right_side), "z")
    live = jnp.arange(tiles.shape[0], dtype=jnp.int32) < tile_count
    tiles = jnp.where(live[:, None, None], tiles, jnp.zeros_like(tiles))
    own = own * (tiles[0, :1, :1] == tiles[0, :1, :1]).astype(jnp.bfloat16)
    slots = tile_rows * COLS + tile_cols
    half, chip = height >> 2, height & 3
    same = (tile_cols >> 2) == half
    apart = jnp.where(same, tile_cols & 3, 3 - (tile_cols & 3)) ^ chip
    place = ((apart & 1) * 2 + (apart >> 1)) * 2 + jnp.where(same, 0, 1)
    last_slots = tile_rows * COLS + place
    levels = jnp.arange(depth_reg.shape[0], dtype=jnp.int32)
    level_hot = (depth_level[:, None] == levels[None, :]).astype(jnp.float32)
    reg_cell = jnp.sum(level_hot * depth_reg[None, :], axis=1)
    reg = jnp.broadcast_to(reg_cell[:, None], (cells, probes))
    sums = call(start_kernel, f32(SUMS, probes), (right_side, reg))
    weights = data_weight.reshape(-1, chunk * PACK)

    def products(own, sums, places):
        total = call(
            forward_own_kernel, f32(group_rows, probes), (core, places, own, tiles), smem=2
        )
        partial = call(
            forward_other_kernel,
            bf16(n_dp, chunk, probes),
            (dp, core, places, swap(own), tiles, total, sums),
            smem=3,
            scratch=[pltpu.VMEM((group_rows, probes), jnp.float32)],
        )
        weighted = call(
            weight_kernel,
            bf16(n_dp, chunk + PARTS, probes),
            (dp, exchange(partial, DP), weights, sums),
            smem=1,
        )
        operands = (core, slots, exchange(weighted, DP), tiles)
        source = pltpu.VMEM((group_rows, probes), jnp.bfloat16)
        rows = n_z * cells
        coded = call(
            backward_send_kernel,
            f32(rows + PARTS + n_z, probes),
            operands,
            smem=2,
            scratch=[source, pltpu.VMEM((rows, probes), jnp.float32)],
        )
        keep, kept_sums = call(
            backward_keep_kernel,
            [f32(rows, probes), f32(SUMS, probes)],
            (*operands, coded),
            smem=2,
            scratch=[source],
        )
        return keep, kept_sums, swap(coded.astype(jnp.float16)).astype(jnp.float32)

    def halved(kernel, blocks, operands, to, smem=0, scratch=()):
        kept, coded, sums = call(
            kernel,
            (f32(blocks * cells, probes), f32(blocks * cells + PARTS, probes), f32(SUMS, probes)),
            operands,
            smem=smem,
            scratch=scratch,
        )
        return kept, along_z(coded.astype(jnp.float16), to).astype(jnp.float32), sums

    whole, extra = f32(cells, probes), f32(SUMS, probes)
    terms = products(own, sums, slots)
    terms = halved(
        spread_kernel,
        4,
        (height, *terms),
        near,
        smem=1,
        scratch=[pltpu.VMEM((n_z * cells, probes), jnp.float32)],
    )
    terms = halved(halve_kernel, 2, terms, far)
    terms = halved(cross_kernel, 2, (*terms, right_side, reg), mirror)
    residual, image, low, sums, keep = call(
        first_update_kernel,
        (whole, whole, bf16(2, cells, probes), extra, extra),
        (height, *terms, own, right_side, reg),
        smem=1,
    )
    low = jnp.concatenate([low, along_z(low, far)], axis=0)
    low = jnp.concatenate([low, along_z(low, near)], axis=0)
    terms = call(pair_kernel, f32(n_z, cells + SUMS, probes), products(low, sums, last_slots))
    got = exchange(terms.astype(jnp.float16), "z").astype(jnp.float32)
    return call(
        last_update_kernel,
        (whole, whole),
        (got, right_side, reg, residual, image, keep),
    )


DP = ("y", "x")


def solution(mesh):
    n_dp, n_mp = mesh.devices.shape
    split_mesh = jax.sharding.Mesh(
        mesh.devices.reshape(n_dp // SIDE, SIDE, n_mp // CORES, CORES), ("y", "x", "z", "core")
    )
    mp = ("z", "core")
    every = DP + mp
    placed = (
        P(every, None, None),
        P(every),
        P(every),
        P(every),
        P(mp),
        P(every),
        P(),
        P(every, None),
    )
    return jax.shard_map(
        body,
        mesh=split_mesh,
        in_specs=placed,
        out_specs=(P(every, None), P(every, None)),
        check_vma=False,
    )
```

```python
import functools

import jax
import jax.numpy as jnp
from jax import lax
from jax.experimental import pallas as pl
from jax.experimental.pallas import tpu as pltpu
from jax.sharding import PartitionSpec as P

SUMS = 8
TERMS = 3
PARTS = 16
CORES = 2
SIDE = 4
KINDS = 3
CELLS = 128
FOUR = 4
COLS = 8
PACK = 2
TOP = 10.0
SUM_TOP = 14.0
VMEM_LIMIT = 16 * 1024 * 1024
VMEM_WHOLE = 60 * 1024 * 1024


def call(kernel, out_shape, operands, smem=0, scratch=(), flops=None):
    spaces = [pltpu.SMEM] * smem + [pltpu.VMEM] * (len(operands) - smem)
    return pl.pallas_call(
        kernel,
        out_shape=out_shape,
        in_specs=[pl.BlockSpec(memory_space=space) for space in spaces],
        out_specs=jax.tree.map(lambda _: pl.BlockSpec(memory_space=pltpu.VMEM), out_shape),
        scratch_shapes=list(scratch),
        cost_estimate=flops and pl.CostEstimate(flops=flops, bytes_accessed=0, transcendentals=0),
        compiler_params=pltpu.CompilerParams(vmem_limit_bytes=VMEM_LIMIT),
    )(*operands)


def f32(*shape):
    return jax.ShapeDtypeStruct(shape, jnp.float32)


def bf16(*shape):
    return jax.ShapeDtypeStruct(shape, jnp.bfloat16)


def rows_of(*sums):
    blank = jnp.zeros((SUMS - len(sums), sums[0].shape[1]), jnp.float32)
    return jnp.concatenate(list(sums) + [blank], axis=0)


def column_sum(value):
    return jnp.sum(value, axis=0, keepdims=True)


def cell_sums(value, reg, image):
    square = value * value
    return rows_of(column_sum(reg * square), column_sum(square), column_sum(value * image))


def copies_kernel(right_in, low_out, right, low, sems):
    load = pltpu.make_async_copy(right_in, right, sems.at[0])
    load.start()
    load.wait()
    low[...] = right[...].astype(jnp.bfloat16)
    stores = [
        pltpu.make_async_copy(low, low_out.at[block], sems.at[block + 1])
        for block in range(low_out.shape[0])
    ]
    for store in stores:
        store.start()
    for store in stores:
        store.wait()


def start_kernel(right_ref, reg_ref, sums_ref):
    right = right_ref[...]
    sums_ref[...] = cell_sums(right, reg_ref[...], jnp.zeros_like(right))


def weight_column(part, weights):
    row = weights[pl.ds(part // PACK, 1), :]
    n = row.shape[1]
    shape = (n // PACK, n)
    wanted = lax.broadcasted_iota(jnp.int32, shape, 0) + lax.rem(part, PACK) * (n // PACK)
    same = lax.broadcasted_iota(jnp.int32, shape, 1) == wanted
    return jnp.sum(jnp.where(same, row, 0.0), axis=1, keepdims=True)


def split(sums):
    left, terms = sums, []
    for _ in range(TERMS):
        high = left.astype(jnp.bfloat16).astype(jnp.float32)
        terms.append(high)
        left = left - high
    return jnp.concatenate(terms, axis=0)


def join(terms):
    return terms[:KINDS] + terms[KINDS : 2 * KINDS] + terms[2 * KINDS : TERMS * KINDS]


def padded(rows):
    if rows.shape[0] == PARTS:
        return rows
    blank = jnp.zeros((PARTS - rows.shape[0], rows.shape[1]), jnp.float32)
    return jnp.concatenate([rows, blank], axis=0)


def exponent(largest):
    return jnp.ceil(jnp.log2(jnp.clip(largest, 1e-30, 1e30)))


def rows_at(start, size):
    return pl.ds(pl.multiple_of(start, size), size)


def row_of(slots, slot):
    return slots[slot] // COLS


def col_of(slots, slot):
    return lax.rem(slots[slot], COLS)


def forward(half, slots, field, tiles, total):
    tile = tiles.shape[1]
    cells = tile // CORES
    for slot in range(tiles.shape[0]):
        total[rows_at(row_of(slots, slot) * tile, tile), :] += jnp.dot(
            tiles[slot, :, rows_at(half * cells, cells)],
            field[col_of(slots, slot)],
            preferred_element_type=jnp.float32,
        )


def forward_own_kernel(core, slots, own, tiles, total):
    total[...] = jnp.zeros_like(total)
    forward(core[0], slots, own, tiles, total)


def forward_other_kernel(dp, core, slots, other, tiles, own_total, sums, out, total):
    chunk = out.shape[1]
    total[...] = own_total[...]
    forward(1 - core[0], slots, other, tiles, total)
    for part in range(out.shape[0]):
        out[part] = total[part * chunk : (part + 1) * chunk].astype(jnp.bfloat16)


def added(got):
    total = got[0].astype(jnp.float32)
    for part in range(1, got.shape[0]):
        total = total + got[part].astype(jnp.float32)
    return total


def weight_kernel(part, got, weights, sums, out):
    chunk = got.shape[1]
    predicted = added(got)
    weighted = (weight_column(part[0], weights) * predicted).astype(jnp.bfloat16)
    curve = column_sum(predicted * weighted.astype(jnp.float32)) + sums[0:1]
    extra = padded(split(jnp.concatenate([curve, sums[1:KINDS]], axis=0))).astype(jnp.bfloat16)
    for part in range(out.shape[0]):
        out[part, :chunk] = weighted
        out[part, chunk:] = extra


def backward(half, slots, got, tiles, source, total, part):
    tile = tiles.shape[1]
    parts, chunk = got.shape[0], got.shape[1] - PARTS
    cells = tile // CORES
    sums = got[0, chunk:].astype(jnp.float32)
    for piece in range(1, parts):
        sums = sums + got[piece, chunk:].astype(jnp.float32)
    for piece in range(parts):
        source[piece * chunk : (piece + 1) * chunk] = got[piece, :chunk]
    total[...] = jnp.zeros_like(total)

    for slot in range(tiles.shape[0]):
        block = col_of(slots, slot)
        if part is not None:
            block = jnp.where(block // FOUR == part, lax.rem(block, FOUR), FOUR)
        total[rows_at(block * cells, cells), :] += lax.dot_general(
            tiles[slot, :, rows_at(half * cells, cells)],
            source[rows_at(row_of(slots, slot) * tile, tile), :],
            (((0,), (0,)), ((), ())),
            preferred_element_type=jnp.float32,
        )
    return join(sums)


def backward_send_kernel(part, core, slots, got, tiles, *refs):
    coded, source, total = refs[-3:]
    sums = backward(1 - core[0], slots, got, tiles, source, total, part)
    cells = tiles.shape[1] // CORES
    powers = []
    blocks = COLS if part is None else FOUR
    for block in range(blocks):
        rows = slice(block * cells, (block + 1) * cells)
        power = exponent(jnp.max(jnp.abs(total[rows]), axis=0, keepdims=True))
        coded[rows] = total[rows] * jnp.exp2(TOP - power)
        powers.append(power)
    sum_power = exponent(jnp.abs(sums))
    terms = split(sums * jnp.exp2(TOP - sum_power))
    tail = padded(jnp.concatenate([terms, sum_power], axis=0))
    powers += [jnp.zeros_like(powers[0])] * (COLS - len(powers))
    if part != 0:
        powers = [tail] + powers
    coded[blocks * cells :] = jnp.concatenate(powers, axis=0)


def backward_keep_kernel(part, core, slots, got, tiles, after, keep, sums_out, source):
    sums = backward(core[0], slots, got, tiles, source, keep, part)
    sums_out[...] = rows_of(*[sums[kind : kind + 1] for kind in range(KINDS)])


def pair_kernel(keep, kept_sums, coded, out):
    blocks = out.shape[0]
    cells = out.shape[1] - SUMS
    tail = coded[blocks * cells :]
    at = TERMS * KINDS
    sums = kept_sums[:KINDS] + join(tail[:at]) * jnp.exp2(tail[at : at + KINDS] - TOP)
    sum_power = exponent(jnp.max(jnp.abs(sums), axis=0, keepdims=True))
    sums = sums * jnp.exp2(SUM_TOP - sum_power)
    high = sums.astype(jnp.bfloat16).astype(jnp.float32)
    for block in range(blocks):
        rows = slice(block * cells, (block + 1) * cells)
        back = jnp.exp2(tail[PARTS + block : PARTS + block + 1] - TOP)
        total = keep[rows] + coded[rows] * back
        power = exponent(jnp.max(jnp.abs(total), axis=0, keepdims=True))
        out[block, :cells] = total * jnp.exp2(TOP - power)
        out[block, cells:] = jnp.concatenate([high, sums - high, sum_power, power], axis=0)


def pair_sum(keep, kept_sums, coded, block, blocks):
    cells = CELLS
    tail = coded[blocks * cells :]
    at = TERMS * KINDS
    sums = kept_sums[:KINDS] + join(tail[:at]) * jnp.exp2(tail[at : at + KINDS] - TOP)
    rows = slice(block * cells, (block + 1) * cells)
    back = jnp.exp2(tail[PARTS + block : PARTS + block + 1] - TOP)
    return keep[rows] + coded[rows] * back, sums


def emit(kept_blocks, sent_blocks, sums, kept, coded, kept_sums):
    cells = CELLS
    powers = []
    for at, block in enumerate(kept_blocks):
        kept[at * cells : (at + 1) * cells] = block
    for at, block in enumerate(sent_blocks):
        power = exponent(jnp.max(jnp.abs(block), axis=0, keepdims=True))
        coded[at * cells : (at + 1) * cells] = block * jnp.exp2(TOP - power)
        powers.append(power)
    power = exponent(jnp.abs(sums))
    terms = split(sums * jnp.exp2(TOP - power))
    coded[len(sent_blocks) * cells :] = padded(jnp.concatenate([terms, power] + powers, axis=0))
    kept_sums[...] = rows_of(*[sums[kind : kind + 1] for kind in range(KINDS)])


def absorb(kept, coded, kept_sums, order):
    cells = CELLS
    tail = coded[kept.shape[0] :]
    at = TERMS * KINDS
    blocks = []
    for block, place in enumerate(order):
        arrived = coded[place * cells : (place + 1) * cells]
        power = tail[at + KINDS + place : at + KINDS + place + 1]
        blocks.append(kept[block * cells : (block + 1) * cells] + arrived * jnp.exp2(power - TOP))
    return blocks, kept_sums[:KINDS] + join(tail[:at]) * jnp.exp2(tail[at : at + KINDS] - TOP)


def spread_kernel(keep, keep_sums, swapped, coded, kept_sums):
    blocks = [pair_sum(keep, keep_sums, swapped, block, FOUR) for block in range(FOUR)]
    emit([], [total for total, _ in blocks], blocks[0][1], None, coded, kept_sums)


def halve_kernel(keep, keep_sums, swapped, coded_in, sums_in, kept, coded, kept_sums, total):
    cells = CELLS
    for block in range(FOUR):
        rows = slice(block * cells, (block + 1) * cells)
        power = swapped[FOUR * cells + block : FOUR * cells + block + 1]
        total[rows] = keep[rows] + swapped[rows] * jnp.exp2(power - TOP)
    blocks, sums = absorb(total, coded_in, sums_in, range(FOUR))
    emit(blocks[:2], blocks[2:], sums, kept, coded, kept_sums)


def cross_kernel(kept_in, coded_in, sums_in, right_ref, reg_ref, kept, coded, kept_sums):
    (own, other), sums = absorb(kept_in, coded_in, sums_in, range(2))
    emit([own, other], [own + reg_ref[...] * right_ref[...], other], sums, kept, coded, kept_sums)


def summed(got, cells):
    total, sums = 0.0, 0.0
    for part in range(got.shape[0]):
        tail = got[part, cells:]
        total = total + got[part, :cells] * jnp.exp2(tail[2 * KINDS + 1 :] - TOP)
        high, low, power = tail[:KINDS], tail[KINDS : 2 * KINDS], tail[2 * KINDS : 2 * KINDS + 1]
        sums = sums + (high + low) * jnp.exp2(power - SUM_TOP)
    return total, sums


def first_update_kernel(
    height, kept, coded, kept_sums, gathered, right_ref, reg_ref, residual_ref, image_ref, low_ref, sums_ref, keep_ref
):
    (terms, other), sums = absorb(kept, coded, kept_sums, (1, 0))
    right, reg = right_ref[...], reg_ref[...]
    curve, norm = sums[0:1], sums[1:2]
    alpha = norm / curve
    image = terms + reg * right
    residual = right - alpha * image
    residual_ref[...] = residual
    image_ref[...] = image
    low_ref[0] = residual.astype(jnp.bfloat16)
    other_right = gathered[COLS - 1 - height[0]].astype(jnp.float32)
    low_ref[1] = (other_right - alpha * other).astype(jnp.bfloat16)
    sums_ref[...] = cell_sums(residual, reg, image)
    keep_ref[...] = rows_of(norm, curve, alpha)


def last_update_kernel(got, right_ref, reg_ref, residual_ref, image_ref, keep_ref, solution_out, residual_out):
    right, residual = right_ref[...], residual_ref[...]
    terms, sums = summed(got, right.shape[0])
    norm, curve, alpha = keep_ref[0:1], keep_ref[1:2], keep_ref[2:3]
    norm_next = sums[1:2]
    ratio = norm_next / norm
    image_next = terms + reg_ref[...] * residual + ratio * image_ref[...]
    curve_next = sums[0:1] + ratio * (2.0 * sums[2:3] + ratio * curve)
    alpha_next = norm_next / curve_next
    direction = residual + ratio * right
    solution_out[...] = alpha * right + alpha_next * direction
    residual_out[...] = residual - alpha_next * image_next


def exchange(value, axis):
    return lax.all_to_all(value, axis, 0, 0)


def along_z(value, to):
    pairs = [
        (z * CORES + core, to(z) * CORES + core)
        for z in range(lax.axis_size("z"))
        for core in range(CORES)
    ]
    return lax.ppermute(value, ("z", "core"), pairs)


def near(z):
    return z ^ 1


def far(z):
    return z ^ 2


def mirror(z):
    return COLS - 1 - z


def swap(value):
    return lax.ppermute(value, "core", [(0, 1), (1, 0)])


def body(tiles, tile_rows, tile_cols, tile_count, data_weight, depth_level, depth_reg, right_side):
    tile = tiles.shape[1]
    cells, probes = right_side.shape
    group_rows = data_weight.shape[0]
    n_dp, n_z = lax.axis_size(DP), lax.axis_size("z")
    chunk = group_rows // n_dp
    col_blocks = cells * CORES * n_z // tile
    core = lax.axis_index("core").astype(jnp.int32).reshape(1)
    height = lax.axis_index("z").astype(jnp.int32).reshape(1)
    dp = lax.axis_index(DP).astype(jnp.int32).reshape(1)

    anywhere = pl.BlockSpec(memory_space=pl.ANY)
    copies = pl.pallas_call(
        copies_kernel,
        out_shape=bf16(n_z, cells, probes),
        in_specs=[anywhere],
        out_specs=anywhere,
        scratch_shapes=[
            pltpu.VMEM((cells, probes), jnp.float32),
            pltpu.VMEM((cells, probes), jnp.bfloat16),
            pltpu.SemaphoreType.DMA((n_z + 1,)),
        ],
        compiler_params=pltpu.CompilerParams(vmem_limit_bytes=VMEM_WHOLE),
    )
    own = exchange(copies(right_side), "z")
    live = jnp.arange(tiles.shape[0], dtype=jnp.int32) < tile_count
    tiles = jnp.where(live[:, None, None], tiles, jnp.zeros_like(tiles))
    own = own * (tiles[0, :1, :1] == tiles[0, :1, :1]).astype(jnp.bfloat16)
    slots = tile_rows * COLS + tile_cols
    half, chip = height >> 2, height & 3
    same = (tile_cols >> 2) == half
    apart = jnp.where(same, tile_cols & 3, 3 - (tile_cols & 3)) ^ chip
    place = ((apart & 1) * 2 + (apart >> 1)) * 2 + jnp.where(same, 0, 1)
    last_slots = tile_rows * COLS + place
    levels = jnp.arange(depth_reg.shape[0], dtype=jnp.int32)
    level_hot = (depth_level[:, None] == levels[None, :]).astype(jnp.float32)
    reg_cell = jnp.sum(level_hot * depth_reg[None, :], axis=1)
    reg = jnp.broadcast_to(reg_cell[:, None], (cells, probes))
    sums = call(start_kernel, f32(SUMS, probes), (right_side, reg))
    weights = data_weight.reshape(-1, chunk * PACK)

    def weighted_data(own, sums, places):
        total = call(
            forward_own_kernel, f32(group_rows, probes), (core, places, own, tiles), smem=2
        )
        partial = call(
            forward_other_kernel,
            bf16(n_dp, chunk, probes),
            (dp, core, places, swap(own), tiles, total, sums),
            smem=3,
            scratch=[pltpu.VMEM((group_rows, probes), jnp.float32)],
        )
        weighted = call(
            weight_kernel,
            bf16(n_dp, chunk + PARTS, probes),
            (dp, exchange(partial, DP), weights, sums),
            smem=1,
        )
        return exchange(weighted, DP)

    def transposed(gathered, places, part=None, after=()):
        operands = (core, places, gathered, tiles)
        source = pltpu.VMEM((group_rows, probes), jnp.bfloat16)
        blocks = n_z if part is None else FOUR
        rows = blocks * cells
        room = rows if part is None else rows + cells
        flops = 2 * tiles.shape[0] * tile * cells * probes
        coded = call(
            functools.partial(backward_send_kernel, part),
            f32(rows + (COLS if part == 0 else PARTS + COLS), probes),
            (*operands, *after),
            smem=2,
            flops=flops,
            scratch=[source, pltpu.VMEM((room, probes), jnp.float32)],
        )
        keep, kept_sums = call(
            functools.partial(backward_keep_kernel, part),
            [f32(room, probes), f32(SUMS, probes)],
            (*operands, coded),
            smem=2,
            flops=flops,
            scratch=[source],
        )
        return keep, kept_sums, swap(coded.astype(jnp.float16)).astype(jnp.float32)

    def sent(coded, to):
        return along_z(coded.astype(jnp.float16), to).astype(jnp.float32)

    whole, extra = f32(cells, probes), f32(SUMS, probes)
    pair, pair_coded = f32(2 * cells, probes), f32(2 * cells + PARTS, probes)
    four_coded = f32(FOUR * cells + PARTS, probes)
    gathered = weighted_data(own, sums, slots)
    coded, sums = call(spread_kernel, (four_coded, extra), transposed(gathered, last_slots, 1))
    stays = transposed(gathered, last_slots, 0, after=(coded,))
    kept, coded, sums = call(
        halve_kernel,
        (pair, pair_coded, extra),
        (*stays, sent(coded, near), sums),
        scratch=[pltpu.VMEM((FOUR * cells, probes), jnp.float32)],
    )
    kept, coded, sums = call(
        cross_kernel, (pair, pair_coded, extra), (kept, sent(coded, far), sums, right_side, reg)
    )
    residual, image, low, sums, keep = call(
        first_update_kernel,
        (whole, whole, bf16(2, cells, probes), extra, extra),
        (height, kept, sent(coded, mirror), sums, own, right_side, reg),
        smem=1,
    )
    low = jnp.concatenate([low, along_z(low, far)], axis=0)
    low = jnp.concatenate([low, along_z(low, near)], axis=0)
    terms = transposed(weighted_data(low, sums, last_slots), slots)
    terms = call(pair_kernel, f32(n_z, cells + SUMS, probes), terms)
    got = exchange(terms.astype(jnp.float16), "z").astype(jnp.float32)
    return call(
        last_update_kernel,
        (whole, whole),
        (got, right_side, reg, residual, image, keep),
    )


DP = ("y", "x")


def solution(mesh):
    n_dp, n_mp = mesh.devices.shape
    split_mesh = jax.sharding.Mesh(
        mesh.devices.reshape(n_dp // SIDE, SIDE, n_mp // CORES, CORES), ("y", "x", "z", "core")
    )
    mp = ("z", "core")
    every = DP + mp
    placed = (
        P(every, None, None),
        P(every),
        P(every),
        P(every),
        P(mp),
        P(every),
        P(),
        P(every, None),
    )
    return jax.shard_map(
        body,
        mesh=split_mesh,
        in_specs=placed,
        out_specs=(P(every, None), P(every, None)),
        check_vma=False,
    )
```

```python
import functools

import jax
import jax.numpy as jnp
from jax import lax
from jax.experimental import pallas as pl
from jax.experimental.pallas import tpu as pltpu
from jax.sharding import PartitionSpec as P

SUMS = 8
TERMS = 3
PARTS = 16
CORES = 2
SIDE = 4
KINDS = 3
CELLS = 128
FOUR = 4
COLS = 8
PACK = 2
TOP = 10.0
SUM_TOP = 14.0
VMEM_LIMIT = 16 * 1024 * 1024
VMEM_WHOLE = 60 * 1024 * 1024


def call(kernel, out_shape, operands, smem=0, scratch=()):
    spaces = [pltpu.SMEM] * smem + [pltpu.VMEM] * (len(operands) - smem)
    return pl.pallas_call(
        kernel,
        out_shape=out_shape,
        in_specs=[pl.BlockSpec(memory_space=space) for space in spaces],
        out_specs=jax.tree.map(lambda _: pl.BlockSpec(memory_space=pltpu.VMEM), out_shape),
        scratch_shapes=list(scratch),
        compiler_params=pltpu.CompilerParams(vmem_limit_bytes=VMEM_LIMIT),
    )(*operands)


def f32(*shape):
    return jax.ShapeDtypeStruct(shape, jnp.float32)


def bf16(*shape):
    return jax.ShapeDtypeStruct(shape, jnp.bfloat16)


def rows_of(*sums):
    blank = jnp.zeros((SUMS - len(sums), sums[0].shape[1]), jnp.float32)
    return jnp.concatenate(list(sums) + [blank], axis=0)


def column_sum(value):
    return jnp.sum(value, axis=0, keepdims=True)


def cell_sums(value, reg, image):
    square = value * value
    return rows_of(column_sum(reg * square), column_sum(square), column_sum(value * image))


def copies_kernel(right_in, low_out, right, low, sems):
    load = pltpu.make_async_copy(right_in, right, sems.at[0])
    load.start()
    load.wait()
    low[...] = right[...].astype(jnp.bfloat16)
    stores = [
        pltpu.make_async_copy(low, low_out.at[block], sems.at[block + 1])
        for block in range(low_out.shape[0])
    ]
    for store in stores:
        store.start()
    for store in stores:
        store.wait()


def start_kernel(right_ref, reg_ref, sums_ref):
    right = right_ref[...]
    sums_ref[...] = cell_sums(right, reg_ref[...], jnp.zeros_like(right))


def weight_column(part, weights):
    row = weights[pl.ds(part // PACK, 1), :]
    n = row.shape[1]
    shape = (n // PACK, n)
    wanted = lax.broadcasted_iota(jnp.int32, shape, 0) + lax.rem(part, PACK) * (n // PACK)
    same = lax.broadcasted_iota(jnp.int32, shape, 1) == wanted
    return jnp.sum(jnp.where(same, row, 0.0), axis=1, keepdims=True)


def split(sums):
    left, terms = sums, []
    for _ in range(TERMS):
        high = left.astype(jnp.bfloat16).astype(jnp.float32)
        terms.append(high)
        left = left - high
    return jnp.concatenate(terms, axis=0)


def join(terms):
    return terms[:KINDS] + terms[KINDS : 2 * KINDS] + terms[2 * KINDS : TERMS * KINDS]


def padded(rows):
    if rows.shape[0] == PARTS:
        return rows
    blank = jnp.zeros((PARTS - rows.shape[0], rows.shape[1]), jnp.float32)
    return jnp.concatenate([rows, blank], axis=0)


def exponent(largest):
    return jnp.ceil(jnp.log2(jnp.clip(largest, 1e-30, 1e30)))


def rows_at(start, size):
    return pl.ds(pl.multiple_of(start, size), size)


def row_of(slots, slot):
    return slots[slot] // COLS


def col_of(slots, slot):
    return lax.rem(slots[slot], COLS)


def forward(half, slots, field, tiles, total):
    tile = tiles.shape[1]
    cells = tile // CORES
    for slot in range(tiles.shape[0]):
        total[rows_at(row_of(slots, slot) * tile, tile), :] += jnp.dot(
            tiles[slot, :, rows_at(half * cells, cells)],
            field[col_of(slots, slot)],
            preferred_element_type=jnp.float32,
        )


def forward_own_kernel(core, slots, own, tiles, total):
    total[...] = jnp.zeros_like(total)
    forward(core[0], slots, own, tiles, total)


def forward_other_kernel(dp, core, slots, other, tiles, own_total, sums, out, total):
    chunk = out.shape[1]
    total[...] = own_total[...]
    forward(1 - core[0], slots, other, tiles, total)
    for part in range(out.shape[0]):
        out[part] = total[part * chunk : (part + 1) * chunk].astype(jnp.bfloat16)


def added(got):
    total = got[0].astype(jnp.float32)
    for part in range(1, got.shape[0]):
        total = total + got[part].astype(jnp.float32)
    return total


def weight_kernel(part, got, weights, sums, out):
    chunk = got.shape[1]
    predicted = added(got)
    weighted = (weight_column(part[0], weights) * predicted).astype(jnp.bfloat16)
    curve = column_sum(predicted * weighted.astype(jnp.float32)) + sums[0:1]
    extra = padded(split(jnp.concatenate([curve, sums[1:KINDS]], axis=0))).astype(jnp.bfloat16)
    for part in range(out.shape[0]):
        out[part, :chunk] = weighted
        out[part, chunk:] = extra


def backward(half, slots, got, tiles, source, total):
    tile = tiles.shape[1]
    parts, chunk = got.shape[0], got.shape[1] - PARTS
    cells = tile // CORES
    sums = got[0, chunk:].astype(jnp.float32)
    for part in range(1, parts):
        sums = sums + got[part, chunk:].astype(jnp.float32)
    for part in range(parts):
        source[part * chunk : (part + 1) * chunk] = got[part, :chunk]
    total[...] = jnp.zeros_like(total)
    for slot in range(tiles.shape[0]):
        total[rows_at(col_of(slots, slot) * cells, cells), :] += lax.dot_general(
            tiles[slot, :, rows_at(half * cells, cells)],
            source[rows_at(row_of(slots, slot) * tile, tile), :],
            (((0,), (0,)), ((), ())),
            preferred_element_type=jnp.float32,
        )
    return join(sums)


def backward_send_kernel(core, slots, got, tiles, coded, source, total):
    sums = backward(1 - core[0], slots, got, tiles, source, total)
    cells = tiles.shape[1] // CORES
    powers = []
    for block in range(total.shape[0] // cells):
        rows = slice(block * cells, (block + 1) * cells)
        power = exponent(jnp.max(jnp.abs(total[rows]), axis=0, keepdims=True))
        coded[rows] = total[rows] * jnp.exp2(TOP - power)
        powers.append(power)
    sum_power = exponent(jnp.abs(sums))
    terms = split(sums * jnp.exp2(TOP - sum_power))
    tail = padded(jnp.concatenate([terms, sum_power], axis=0))
    coded[total.shape[0] :] = jnp.concatenate([tail] + powers, axis=0)


def backward_keep_kernel(core, slots, got, tiles, after, keep, sums_out, source):
    sums = backward(core[0], slots, got, tiles, source, keep)
    sums_out[...] = rows_of(*[sums[kind : kind + 1] for kind in range(KINDS)])


def pair_kernel(keep, kept_sums, coded, out):
    blocks = out.shape[0]
    cells = out.shape[1] - SUMS
    tail = coded[blocks * cells :]
    at = TERMS * KINDS
    sums = kept_sums[:KINDS] + join(tail[:at]) * jnp.exp2(tail[at : at + KINDS] - TOP)
    sum_power = exponent(jnp.max(jnp.abs(sums), axis=0, keepdims=True))
    sums = sums * jnp.exp2(SUM_TOP - sum_power)
    high = sums.astype(jnp.bfloat16).astype(jnp.float32)
    for block in range(blocks):
        rows = slice(block * cells, (block + 1) * cells)
        back = jnp.exp2(tail[PARTS + block : PARTS + block + 1] - TOP)
        total = keep[rows] + coded[rows] * back
        power = exponent(jnp.max(jnp.abs(total), axis=0, keepdims=True))
        out[block, :cells] = total * jnp.exp2(TOP - power)
        out[block, cells:] = jnp.concatenate([high, sums - high, sum_power, power], axis=0)


def pair_sum(keep, kept_sums, coded, block):
    cells = CELLS
    blocks = keep.shape[0] // cells
    tail = coded[blocks * cells :]
    at = TERMS * KINDS
    sums = kept_sums[:KINDS] + join(tail[:at]) * jnp.exp2(tail[at : at + KINDS] - TOP)
    rows = slice(block * cells, (block + 1) * cells)
    back = jnp.exp2(tail[PARTS + block : PARTS + block + 1] - TOP)
    return keep[rows] + coded[rows] * back, sums


def emit(kept_blocks, sent_blocks, sums, kept, coded, kept_sums):
    cells = CELLS
    powers = []
    for at, block in enumerate(kept_blocks):
        kept[at * cells : (at + 1) * cells] = block
    for at, block in enumerate(sent_blocks):
        power = exponent(jnp.max(jnp.abs(block), axis=0, keepdims=True))
        coded[at * cells : (at + 1) * cells] = block * jnp.exp2(TOP - power)
        powers.append(power)
    power = exponent(jnp.abs(sums))
    terms = split(sums * jnp.exp2(TOP - power))
    coded[len(sent_blocks) * cells :] = padded(jnp.concatenate([terms, power] + powers, axis=0))
    kept_sums[...] = rows_of(*[sums[kind : kind + 1] for kind in range(KINDS)])


def absorb(kept, coded, kept_sums, order):
    cells = CELLS
    tail = coded[kept.shape[0] :]
    at = TERMS * KINDS
    blocks = []
    for block, place in enumerate(order):
        arrived = coded[place * cells : (place + 1) * cells]
        power = tail[at + KINDS + place : at + KINDS + place + 1]
        blocks.append(kept[block * cells : (block + 1) * cells] + arrived * jnp.exp2(power - TOP))
    return blocks, kept_sums[:KINDS] + join(tail[:at]) * jnp.exp2(tail[at : at + KINDS] - TOP)


def spread_kernel(height, keep, keep_sums, swapped, kept, coded, kept_sums, total):
    cells = CELLS
    for block in range(COLS):
        part, sums = pair_sum(keep, keep_sums, swapped, block)
        total[block * cells : (block + 1) * cells] = part
    half, own = height[0] // FOUR, lax.rem(height[0], FOUR)

    def blocks(chips):
        at = [z for chip in chips for z in (half * FOUR + chip, (2 - half) * FOUR - 1 - chip)]
        return [total[rows_at(z * cells, cells), :] for z in at]

    emit(
        blocks([own, jnp.bitwise_xor(own, 2)]),
        blocks([jnp.bitwise_xor(own, 1), jnp.bitwise_xor(own, 3)]),
        sums,
        kept,
        coded,
        kept_sums,
    )


def halve_kernel(kept_in, coded_in, sums_in, kept, coded, kept_sums):
    blocks, sums = absorb(kept_in, coded_in, sums_in, range(4))
    emit(blocks[:2], blocks[2:], sums, kept, coded, kept_sums)


def cross_kernel(kept_in, coded_in, sums_in, right_ref, reg_ref, kept, coded, kept_sums):
    (own, other), sums = absorb(kept_in, coded_in, sums_in, range(2))
    emit([own, other], [own + reg_ref[...] * right_ref[...], other], sums, kept, coded, kept_sums)


def summed(got, cells):
    total, sums = 0.0, 0.0
    for part in range(got.shape[0]):
        tail = got[part, cells:]
        total = total + got[part, :cells] * jnp.exp2(tail[2 * KINDS + 1 :] - TOP)
        high, low, power = tail[:KINDS], tail[KINDS : 2 * KINDS], tail[2 * KINDS : 2 * KINDS + 1]
        sums = sums + (high + low) * jnp.exp2(power - SUM_TOP)
    return total, sums


def first_update_kernel(
    height, kept, coded, kept_sums, gathered, right_ref, reg_ref, residual_ref, image_ref, low_ref, sums_ref, keep_ref
):
    (terms, other), sums = absorb(kept, coded, kept_sums, (1, 0))
    right, reg = right_ref[...], reg_ref[...]
    curve, norm = sums[0:1], sums[1:2]
    alpha = norm / curve
    image = terms + reg * right
    residual = right - alpha * image
    residual_ref[...] = residual
    image_ref[...] = image
    low_ref[0] = residual.astype(jnp.bfloat16)
    other_right = gathered[COLS - 1 - height[0]].astype(jnp.float32)
    low_ref[1] = (other_right - alpha * other).astype(jnp.bfloat16)
    sums_ref[...] = cell_sums(residual, reg, image)
    keep_ref[...] = rows_of(norm, curve, alpha)


def last_update_kernel(got, right_ref, reg_ref, residual_ref, image_ref, keep_ref, solution_out, residual_out):
    right, residual = right_ref[...], residual_ref[...]
    terms, sums = summed(got, right.shape[0])
    norm, curve, alpha = keep_ref[0:1], keep_ref[1:2], keep_ref[2:3]
    norm_next = sums[1:2]
    ratio = norm_next / norm
    image_next = terms + reg_ref[...] * residual + ratio * image_ref[...]
    curve_next = sums[0:1] + ratio * (2.0 * sums[2:3] + ratio * curve)
    alpha_next = norm_next / curve_next
    direction = residual + ratio * right
    solution_out[...] = alpha * right + alpha_next * direction
    residual_out[...] = residual - alpha_next * image_next


def exchange(value, axis):
    return lax.all_to_all(value, axis, 0, 0)


def along_z(value, to):
    pairs = [
        (z * CORES + core, to(z) * CORES + core)
        for z in range(lax.axis_size("z"))
        for core in range(CORES)
    ]
    return lax.ppermute(value, ("z", "core"), pairs)


def near(z):
    return z ^ 1


def far(z):
    return z ^ 2


def mirror(z):
    return COLS - 1 - z


def swap(value):
    return lax.ppermute(value, "core", [(0, 1), (1, 0)])


def body(tiles, tile_rows, tile_cols, tile_count, data_weight, depth_level, depth_reg, right_side):
    tile = tiles.shape[1]
    cells, probes = right_side.shape
    group_rows = data_weight.shape[0]
    n_dp, n_z = lax.axis_size(DP), lax.axis_size("z")
    chunk = group_rows // n_dp
    col_blocks = cells * CORES * n_z // tile
    core = lax.axis_index("core").astype(jnp.int32).reshape(1)
    height = lax.axis_index("z").astype(jnp.int32).reshape(1)
    dp = lax.axis_index(DP).astype(jnp.int32).reshape(1)

    anywhere = pl.BlockSpec(memory_space=pl.ANY)
    copies = pl.pallas_call(
        copies_kernel,
        out_shape=bf16(n_z, cells, probes),
        in_specs=[anywhere],
        out_specs=anywhere,
        scratch_shapes=[
            pltpu.VMEM((cells, probes), jnp.float32),
            pltpu.VMEM((cells, probes), jnp.bfloat16),
            pltpu.SemaphoreType.DMA((n_z + 1,)),
        ],
        compiler_params=pltpu.CompilerParams(vmem_limit_bytes=VMEM_WHOLE),
    )
    own = exchange(copies(right_side), "z")
    live = jnp.arange(tiles.shape[0], dtype=jnp.int32) < tile_count
    tiles = jnp.where(live[:, None, None], tiles, jnp.zeros_like(tiles))
    own = own * (tiles[0, :1, :1] == tiles[0, :1, :1]).astype(jnp.bfloat16)
    slots = tile_rows * COLS + tile_cols
    half, chip = height >> 2, height & 3
    same = (tile_cols >> 2) == half
    apart = jnp.where(same, tile_cols & 3, 3 - (tile_cols & 3)) ^ chip
    place = ((apart & 1) * 2 + (apart >> 1)) * 2 + jnp.where(same, 0, 1)
    last_slots = tile_rows * COLS + place
    levels = jnp.arange(depth_reg.shape[0], dtype=jnp.int32)
    level_hot = (depth_level[:, None] == levels[None, :]).astype(jnp.float32)
    reg_cell = jnp.sum(level_hot * depth_reg[None, :], axis=1)
    reg = jnp.broadcast_to(reg_cell[:, None], (cells, probes))
    sums = call(start_kernel, f32(SUMS, probes), (right_side, reg))
    weights = data_weight.reshape(-1, chunk * PACK)

    def products(own, other, sums, places):
        total = call(
            forward_own_kernel, f32(group_rows, probes), (core, places, own, tiles), smem=2
        )
        partial = call(
            forward_other_kernel,
            bf16(n_dp, chunk, probes),
            (dp, core, places, other, tiles, total, sums),
            smem=3,
            scratch=[pltpu.VMEM((group_rows, probes), jnp.float32)],
        )
        weighted = call(
            weight_kernel,
            bf16(n_dp, chunk + PARTS, probes),
            (dp, exchange(partial, DP), weights, sums),
            smem=1,
        )
        operands = (core, slots, exchange(weighted, DP), tiles)
        source = pltpu.VMEM((group_rows, probes), jnp.bfloat16)
        rows = n_z * cells
        coded = call(
            backward_send_kernel,
            f32(rows + PARTS + n_z, probes),
            operands,
            smem=2,
            scratch=[source, pltpu.VMEM((rows, probes), jnp.float32)],
        )
        keep, kept_sums = call(
            backward_keep_kernel,
            [f32(rows, probes), f32(SUMS, probes)],
            (*operands, coded),
            smem=2,
            scratch=[source],
        )
        return keep, kept_sums, swap(coded.astype(jnp.float16)).astype(jnp.float32)

    def halved(kernel, blocks, operands, to, smem=0, scratch=()):
        kept, coded, sums = call(
            kernel,
            (f32(blocks * cells, probes), f32(blocks * cells + PARTS, probes), f32(SUMS, probes)),
            operands,
            smem=smem,
            scratch=scratch,
        )
        return kept, along_z(coded.astype(jnp.float16), to).astype(jnp.float32), sums

    whole, extra = f32(cells, probes), f32(SUMS, probes)
    terms = products(own, swap(own), sums, slots)
    terms = halved(
        spread_kernel,
        4,
        (height, *terms),
        near,
        smem=1,
        scratch=[pltpu.VMEM((n_z * cells, probes), jnp.float32)],
    )
    terms = halved(halve_kernel, 2, terms, far)
    terms = halved(cross_kernel, 2, (*terms, right_side, reg), mirror)
    residual, image, low, sums, keep = call(
        first_update_kernel,
        (whole, whole, bf16(2, cells, probes), extra, extra),
        (height, *terms, own, right_side, reg),
        smem=1,
    )
    low = jnp.concatenate([low, along_z(low, far)], axis=0)
    later = along_z(low, near)
    other = jnp.concatenate([swap(low), swap(later)], axis=0)
    low = jnp.concatenate([low, later], axis=0)
    terms = call(pair_kernel, f32(n_z, cells + SUMS, probes), products(low, other, sums, last_slots))
    got = exchange(terms.astype(jnp.float16), "z").astype(jnp.float32)
    return call(
        last_update_kernel,
        (whole, whole),
        (got, right_side, reg, residual, image, keep),
    )


DP = ("y", "x")


def solution(mesh):
    n_dp, n_mp = mesh.devices.shape
    split_mesh = jax.sharding.Mesh(
        mesh.devices.reshape(n_dp // SIDE, SIDE, n_mp // CORES, CORES), ("y", "x", "z", "core")
    )
    mp = ("z", "core")
    every = DP + mp
    placed = (
        P(every, None, None),
        P(every),
        P(every),
        P(every),
        P(mp),
        P(every),
        P(),
        P(every, None),
    )
    return jax.shard_map(
        body,
        mesh=split_mesh,
        in_specs=placed,
        out_specs=(P(every, None), P(every, None)),
        check_vma=False,
    )
```

```python
import functools

import jax
import jax.numpy as jnp
from jax import lax
from jax.experimental import pallas as pl
from jax.experimental.pallas import tpu as pltpu
from jax.sharding import PartitionSpec as P

SUMS = 8
TERMS = 3
PARTS = 16
CORES = 2
SIDE = 4
KINDS = 3
CELLS = 128
FOUR = 4
COLS = 8
PACK = 2
TOP = 10.0
SUM_TOP = 14.0
VMEM_LIMIT = 16 * 1024 * 1024


def call(kernel, out_shape, operands, smem=0, scratch=()):
    spaces = [pltpu.SMEM] * smem + [pltpu.VMEM] * (len(operands) - smem)
    return pl.pallas_call(
        kernel,
        out_shape=out_shape,
        in_specs=[pl.BlockSpec(memory_space=space) for space in spaces],
        out_specs=jax.tree.map(lambda _: pl.BlockSpec(memory_space=pltpu.VMEM), out_shape),
        scratch_shapes=list(scratch),
        compiler_params=pltpu.CompilerParams(vmem_limit_bytes=VMEM_LIMIT),
    )(*operands)


def f32(*shape):
    return jax.ShapeDtypeStruct(shape, jnp.float32)


def bf16(*shape):
    return jax.ShapeDtypeStruct(shape, jnp.bfloat16)


def rows_of(*sums):
    blank = jnp.zeros((SUMS - len(sums), sums[0].shape[1]), jnp.float32)
    return jnp.concatenate(list(sums) + [blank], axis=0)


def column_sum(value):
    return jnp.sum(value, axis=0, keepdims=True)


def cell_sums(value, reg, image):
    square = value * value
    return rows_of(column_sum(reg * square), column_sum(square), column_sum(value * image))


def copies_kernel(right_ref, low_ref):
    low = right_ref[...].astype(jnp.bfloat16)
    for block in range(low_ref.shape[0]):
        low_ref[block] = low


def start_kernel(right_ref, reg_ref, sums_ref):
    right = right_ref[...]
    sums_ref[...] = cell_sums(right, reg_ref[...], jnp.zeros_like(right))


def weight_column(part, weights):
    row = weights[pl.ds(part // PACK, 1), :]
    n = row.shape[1]
    shape = (n // PACK, n)
    wanted = lax.broadcasted_iota(jnp.int32, shape, 0) + lax.rem(part, PACK) * (n // PACK)
    same = lax.broadcasted_iota(jnp.int32, shape, 1) == wanted
    return jnp.sum(jnp.where(same, row, 0.0), axis=1, keepdims=True)


def split(sums):
    left, terms = sums, []
    for _ in range(TERMS):
        high = left.astype(jnp.bfloat16).astype(jnp.float32)
        terms.append(high)
        left = left - high
    return jnp.concatenate(terms, axis=0)


def join(terms):
    return terms[:KINDS] + terms[KINDS : 2 * KINDS] + terms[2 * KINDS : TERMS * KINDS]


def padded(rows):
    if rows.shape[0] == PARTS:
        return rows
    blank = jnp.zeros((PARTS - rows.shape[0], rows.shape[1]), jnp.float32)
    return jnp.concatenate([rows, blank], axis=0)


def exponent(largest):
    return jnp.ceil(jnp.log2(jnp.clip(largest, 1e-30, 1e30)))


def rows_at(start, size):
    return pl.ds(pl.multiple_of(start, size), size)


def row_of(slots, slot):
    return slots[slot] // COLS


def col_of(slots, slot):
    return lax.rem(slots[slot], COLS)


def forward(half, slots, field, tiles, total):
    tile = tiles.shape[1]
    cells = tile // CORES
    for slot in range(tiles.shape[0]):
        total[rows_at(row_of(slots, slot) * tile, tile), :] += jnp.dot(
            tiles[slot, :, rows_at(half * cells, cells)],
            field[col_of(slots, slot)],
            preferred_element_type=jnp.float32,
        )


def forward_own_kernel(core, slots, own, tiles, total):
    total[...] = jnp.zeros_like(total)
    forward(core[0], slots, own, tiles, total)


def forward_other_kernel(dp, core, slots, other, tiles, own_total, sums, out, total):
    chunk = out.shape[1]
    total[...] = own_total[...]
    forward(1 - core[0], slots, other, tiles, total)
    for part in range(out.shape[0]):
        out[part] = total[part * chunk : (part + 1) * chunk].astype(jnp.bfloat16)


def added(got):
    total = got[0].astype(jnp.float32)
    for part in range(1, got.shape[0]):
        total = total + got[part].astype(jnp.float32)
    return total


def weight_kernel(part, got, weights, sums, out):
    chunk = got.shape[1]
    predicted = added(got)
    weighted = (weight_column(part[0], weights) * predicted).astype(jnp.bfloat16)
    curve = column_sum(predicted * weighted.astype(jnp.float32)) + sums[0:1]
    extra = padded(split(jnp.concatenate([curve, sums[1:KINDS]], axis=0))).astype(jnp.bfloat16)
    for part in range(out.shape[0]):
        out[part, :chunk] = weighted
        out[part, chunk:] = extra


def backward(half, slots, got, tiles, source, total):
    tile = tiles.shape[1]
    parts, chunk = got.shape[0], got.shape[1] - PARTS
    cells = tile // CORES
    sums = got[0, chunk:].astype(jnp.float32)
    for part in range(1, parts):
        sums = sums + got[part, chunk:].astype(jnp.float32)
    for part in range(parts):
        source[part * chunk : (part + 1) * chunk] = got[part, :chunk]
    total[...] = jnp.zeros_like(total)
    for slot in range(tiles.shape[0]):
        total[rows_at(col_of(slots, slot) * cells, cells), :] += lax.dot_general(
            tiles[slot, :, rows_at(half * cells, cells)],
            source[rows_at(row_of(slots, slot) * tile, tile), :],
            (((0,), (0,)), ((), ())),
            preferred_element_type=jnp.float32,
        )
    return join(sums)


def backward_send_kernel(core, slots, got, tiles, coded, source, total):
    sums = backward(1 - core[0], slots, got, tiles, source, total)
    cells = tiles.shape[1] // CORES
    powers = []
    for block in range(total.shape[0] // cells):
        rows = slice(block * cells, (block + 1) * cells)
        power = exponent(jnp.max(jnp.abs(total[rows]), axis=0, keepdims=True))
        coded[rows] = total[rows] * jnp.exp2(TOP - power)
        powers.append(power)
    sum_power = exponent(jnp.abs(sums))
    terms = split(sums * jnp.exp2(TOP - sum_power))
    tail = padded(jnp.concatenate([terms, sum_power], axis=0))
    coded[total.shape[0] :] = jnp.concatenate([tail] + powers, axis=0)


def backward_keep_kernel(core, slots, got, tiles, after, keep, sums_out, source):
    sums = backward(core[0], slots, got, tiles, source, keep)
    sums_out[...] = rows_of(*[sums[kind : kind + 1] for kind in range(KINDS)])


def pair_kernel(keep, kept_sums, coded, out):
    blocks = out.shape[0]
    cells = out.shape[1] - SUMS
    tail = coded[blocks * cells :]
    at = TERMS * KINDS
    sums = kept_sums[:KINDS] + join(tail[:at]) * jnp.exp2(tail[at : at + KINDS] - TOP)
    sum_power = exponent(jnp.max(jnp.abs(sums), axis=0, keepdims=True))
    sums = sums * jnp.exp2(SUM_TOP - sum_power)
    high = sums.astype(jnp.bfloat16).astype(jnp.float32)
    for block in range(blocks):
        rows = slice(block * cells, (block + 1) * cells)
        back = jnp.exp2(tail[PARTS + block : PARTS + block + 1] - TOP)
        total = keep[rows] + coded[rows] * back
        power = exponent(jnp.max(jnp.abs(total), axis=0, keepdims=True))
        out[block, :cells] = total * jnp.exp2(TOP - power)
        out[block, cells:] = jnp.concatenate([high, sums - high, sum_power, power], axis=0)


def pair_sum(keep, kept_sums, coded, block):
    cells = CELLS
    blocks = keep.shape[0] // cells
    tail = coded[blocks * cells :]
    at = TERMS * KINDS
    sums = kept_sums[:KINDS] + join(tail[:at]) * jnp.exp2(tail[at : at + KINDS] - TOP)
    rows = slice(block * cells, (block + 1) * cells)
    back = jnp.exp2(tail[PARTS + block : PARTS + block + 1] - TOP)
    return keep[rows] + coded[rows] * back, sums


def emit(kept_blocks, sent_blocks, sums, kept, coded, kept_sums):
    cells = CELLS
    powers = []
    for at, block in enumerate(kept_blocks):
        kept[at * cells : (at + 1) * cells] = block
    for at, block in enumerate(sent_blocks):
        power = exponent(jnp.max(jnp.abs(block), axis=0, keepdims=True))
        coded[at * cells : (at + 1) * cells] = block * jnp.exp2(TOP - power)
        powers.append(power)
    power = exponent(jnp.abs(sums))
    terms = split(sums * jnp.exp2(TOP - power))
    coded[len(sent_blocks) * cells :] = padded(jnp.concatenate([terms, power] + powers, axis=0))
    kept_sums[...] = rows_of(*[sums[kind : kind + 1] for kind in range(KINDS)])


def absorb(kept, coded, kept_sums, order):
    cells = CELLS
    tail = coded[kept.shape[0] :]
    at = TERMS * KINDS
    blocks = []
    for block, place in enumerate(order):
        arrived = coded[place * cells : (place + 1) * cells]
        power = tail[at + KINDS + place : at + KINDS + place + 1]
        blocks.append(kept[block * cells : (block + 1) * cells] + arrived * jnp.exp2(power - TOP))
    return blocks, kept_sums[:KINDS] + join(tail[:at]) * jnp.exp2(tail[at : at + KINDS] - TOP)


def spread_kernel(core, height, keep, keep_sums, swapped, kept, coded, kept_sums, total):
    cells = CELLS
    for block in range(COLS):
        part, sums = pair_sum(keep, keep_sums, swapped, block)
        total[block * cells : (block + 1) * cells] = part
    half, own = height[0] // FOUR, lax.rem(height[0], FOUR)

    def blocks(chips):
        at = [z for chip in chips for z in (half * FOUR + chip, (2 - half) * FOUR - 1 - chip)]
        return [total[rows_at(z * cells, cells), :] for z in at]

    emit(
        blocks([own, jnp.bitwise_xor(own, 2 - core[0])]),
        blocks([jnp.bitwise_xor(own, 1 + core[0]), jnp.bitwise_xor(own, 3)]),
        sums,
        kept,
        coded,
        kept_sums,
    )


def halve_kernel(kept_in, coded_in, sums_in, kept, coded, kept_sums):
    blocks, sums = absorb(kept_in, coded_in, sums_in, range(4))
    emit(blocks[:2], blocks[2:], sums, kept, coded, kept_sums)


def cross_kernel(kept_in, coded_in, sums_in, right_ref, reg_ref, kept, coded, kept_sums):
    (own, other), sums = absorb(kept_in, coded_in, sums_in, range(2))
    emit([own, other], [own + reg_ref[...] * right_ref[...], other], sums, kept, coded, kept_sums)


def summed(got, cells):
    total, sums = 0.0, 0.0
    for part in range(got.shape[0]):
        tail = got[part, cells:]
        total = total + got[part, :cells] * jnp.exp2(tail[2 * KINDS + 1 :] - TOP)
        high, low, power = tail[:KINDS], tail[KINDS : 2 * KINDS], tail[2 * KINDS : 2 * KINDS + 1]
        sums = sums + (high + low) * jnp.exp2(power - SUM_TOP)
    return total, sums


def first_update_kernel(
    height, kept, coded, kept_sums, gathered, right_ref, reg_ref, residual_ref, image_ref, low_ref, sums_ref, keep_ref
):
    (terms, other), sums = absorb(kept, coded, kept_sums, (1, 0))
    right, reg = right_ref[...], reg_ref[...]
    curve, norm = sums[0:1], sums[1:2]
    alpha = norm / curve
    image = terms + reg * right
    residual = right - alpha * image
    residual_ref[...] = residual
    image_ref[...] = image
    low_ref[0] = residual.astype(jnp.bfloat16)
    other_right = gathered[COLS - 1 - height[0]].astype(jnp.float32)
    low_ref[1] = (other_right - alpha * other).astype(jnp.bfloat16)
    sums_ref[...] = cell_sums(residual, reg, image)
    keep_ref[...] = rows_of(norm, curve, alpha)


def last_update_kernel(got, right_ref, reg_ref, residual_ref, image_ref, keep_ref, solution_out, residual_out):
    right, residual = right_ref[...], residual_ref[...]
    terms, sums = summed(got, right.shape[0])
    norm, curve, alpha = keep_ref[0:1], keep_ref[1:2], keep_ref[2:3]
    norm_next = sums[1:2]
    ratio = norm_next / norm
    image_next = terms + reg_ref[...] * residual + ratio * image_ref[...]
    curve_next = sums[0:1] + ratio * (2.0 * sums[2:3] + ratio * curve)
    alpha_next = norm_next / curve_next
    direction = residual + ratio * right
    solution_out[...] = alpha * right + alpha_next * direction
    residual_out[...] = residual - alpha_next * image_next


def exchange(value, axis):
    return lax.all_to_all(value, axis, 0, 0)


def along_z(value, to):
    pairs = [
        (z * CORES + core, to(z, core) * CORES + core)
        for z in range(lax.axis_size("z"))
        for core in range(CORES)
    ]
    return lax.ppermute(value, ("z", "core"), pairs)


def near(z, core):
    return z ^ 1


def far(z, core):
    return z ^ 2


def first(z, core):
    return z ^ (1 + core)


def second(z, core):
    return z ^ (2 - core)


def mirror(z, core):
    return COLS - 1 - z


def swap(value):
    return lax.ppermute(value, "core", [(0, 1), (1, 0)])


def body(tiles, tile_rows, tile_cols, tile_count, data_weight, depth_level, depth_reg, right_side):
    tile = tiles.shape[1]
    cells, probes = right_side.shape
    group_rows = data_weight.shape[0]
    n_dp, n_z = lax.axis_size(DP), lax.axis_size("z")
    chunk = group_rows // n_dp
    col_blocks = cells * CORES * n_z // tile
    core = lax.axis_index("core").astype(jnp.int32).reshape(1)
    height = lax.axis_index("z").astype(jnp.int32).reshape(1)
    dp = lax.axis_index(DP).astype(jnp.int32).reshape(1)

    copies = call(copies_kernel, bf16(n_z, cells, probes), (right_side,))
    own = exchange(copies, "z")
    live = jnp.arange(tiles.shape[0], dtype=jnp.int32) < tile_count
    tiles = jnp.where(live[:, None, None], tiles, jnp.zeros_like(tiles))
    own = own * (tiles[0, :1, :1] == tiles[0, :1, :1]).astype(jnp.bfloat16)
    slots = tile_rows * COLS + tile_cols
    half, chip = height >> 2, height & 3
    same = (tile_cols >> 2) == half
    apart = jnp.where(same, tile_cols & 3, 3 - (tile_cols & 3)) ^ chip
    place = ((apart & 1) * 2 + (apart >> 1)) * 2 + jnp.where(same, 0, 1)
    last_slots = tile_rows * COLS + place
    levels = jnp.arange(depth_reg.shape[0], dtype=jnp.int32)
    level_hot = (depth_level[:, None] == levels[None, :]).astype(jnp.float32)
    reg_cell = jnp.sum(level_hot * depth_reg[None, :], axis=1)
    reg = jnp.broadcast_to(reg_cell[:, None], (cells, probes))
    sums = call(start_kernel, f32(SUMS, probes), (right_side, reg))
    weights = data_weight.reshape(-1, chunk * PACK)

    def products(own, other, sums, places):
        total = call(
            forward_own_kernel, f32(group_rows, probes), (core, places, own, tiles), smem=2
        )
        partial = call(
            forward_other_kernel,
            bf16(n_dp, chunk, probes),
            (dp, core, places, other, tiles, total, sums),
            smem=3,
            scratch=[pltpu.VMEM((group_rows, probes), jnp.float32)],
        )
        weighted = call(
            weight_kernel,
            bf16(n_dp, chunk + PARTS, probes),
            (dp, exchange(partial, DP), weights, sums),
            smem=1,
        )
        operands = (core, slots, exchange(weighted, DP), tiles)
        source = pltpu.VMEM((group_rows, probes), jnp.bfloat16)
        rows = n_z * cells
        coded = call(
            backward_send_kernel,
            f32(rows + PARTS + n_z, probes),
            operands,
            smem=2,
            scratch=[source, pltpu.VMEM((rows, probes), jnp.float32)],
        )
        keep, kept_sums = call(
            backward_keep_kernel,
            [f32(rows, probes), f32(SUMS, probes)],
            (*operands, coded),
            smem=2,
            scratch=[source],
        )
        return keep, kept_sums, swap(coded.astype(jnp.float16)).astype(jnp.float32)

    def halved(kernel, blocks, operands, to, smem=0, scratch=()):
        kept, coded, sums = call(
            kernel,
            (f32(blocks * cells, probes), f32(blocks * cells + PARTS, probes), f32(SUMS, probes)),
            operands,
            smem=smem,
            scratch=scratch,
        )
        return kept, along_z(coded.astype(jnp.float16), to).astype(jnp.float32), sums

    whole, extra = f32(cells, probes), f32(SUMS, probes)
    terms = products(own, swap(own), sums, slots)
    terms = halved(
        spread_kernel,
        4,
        (core, height, *terms),
        first,
        smem=2,
        scratch=[pltpu.VMEM((n_z * cells, probes), jnp.float32)],
    )
    terms = halved(halve_kernel, 2, terms, second)
    terms = halved(cross_kernel, 2, (*terms, right_side, reg), mirror)
    residual, image, low, sums, keep = call(
        first_update_kernel,
        (whole, whole, bf16(2, cells, probes), extra, extra),
        (height, *terms, own, right_side, reg),
        smem=1,
    )
    low = jnp.concatenate([low, along_z(low, far)], axis=0)
    later = along_z(low, near)
    other = jnp.concatenate([swap(low), swap(later)], axis=0)
    low = jnp.concatenate([low, later], axis=0)
    terms = call(pair_kernel, f32(n_z, cells + SUMS, probes), products(low, other, sums, last_slots))
    got = exchange(terms.astype(jnp.float16), "z").astype(jnp.float32)
    return call(
        last_update_kernel,
        (whole, whole),
        (got, right_side, reg, residual, image, keep),
    )


DP = ("y", "x")


def solution(mesh):
    n_dp, n_mp = mesh.devices.shape
    split_mesh = jax.sharding.Mesh(
        mesh.devices.reshape(n_dp // SIDE, SIDE, n_mp // CORES, CORES), ("y", "x", "z", "core")
    )
    mp = ("z", "core")
    every = DP + mp
    placed = (
        P(every, None, None),
        P(every),
        P(every),
        P(every),
        P(mp),
        P(every),
        P(),
        P(every, None),
    )
    return jax.shard_map(
        body,
        mesh=split_mesh,
        in_specs=placed,
        out_specs=(P(every, None), P(every, None)),
        check_vma=False,
    )
```

```python
import functools

import jax
import jax.numpy as jnp
from jax import lax
from jax.experimental import pallas as pl
from jax.experimental.pallas import tpu as pltpu
from jax.sharding import PartitionSpec as P

SUMS = 8
TERMS = 3
PARTS = 16
CORES = 2
SIDE = 4
KINDS = 3
CELLS = 128
FOUR = 4
COLS = 8
PACK = 2
TOP = 10.0
SUM_TOP = 14.0
VMEM_LIMIT = 16 * 1024 * 1024


def call(kernel, out_shape, operands, smem=0, scratch=()):
    spaces = [pltpu.SMEM] * smem + [pltpu.VMEM] * (len(operands) - smem)
    return pl.pallas_call(
        kernel,
        out_shape=out_shape,
        in_specs=[pl.BlockSpec(memory_space=space) for space in spaces],
        out_specs=jax.tree.map(lambda _: pl.BlockSpec(memory_space=pltpu.VMEM), out_shape),
        scratch_shapes=list(scratch),
        compiler_params=pltpu.CompilerParams(vmem_limit_bytes=VMEM_LIMIT),
    )(*operands)


def f32(*shape):
    return jax.ShapeDtypeStruct(shape, jnp.float32)


def bf16(*shape):
    return jax.ShapeDtypeStruct(shape, jnp.bfloat16)


def rows_of(*sums):
    blank = jnp.zeros((SUMS - len(sums), sums[0].shape[1]), jnp.float32)
    return jnp.concatenate(list(sums) + [blank], axis=0)


def column_sum(value):
    return jnp.sum(value, axis=0, keepdims=True)


def cell_sums(value, reg, image):
    square = value * value
    return rows_of(column_sum(reg * square), column_sum(square), column_sum(value * image))


def copies_kernel(right_ref, low_ref):
    low = right_ref[...].astype(jnp.bfloat16)
    for block in range(low_ref.shape[0]):
        low_ref[block] = low


def start_kernel(right_ref, reg_ref, sums_ref):
    right = right_ref[...]
    sums_ref[...] = cell_sums(right, reg_ref[...], jnp.zeros_like(right))


def weight_column(part, weights):
    row = weights[pl.ds(part // PACK, 1), :]
    n = row.shape[1]
    shape = (n // PACK, n)
    wanted = lax.broadcasted_iota(jnp.int32, shape, 0) + lax.rem(part, PACK) * (n // PACK)
    same = lax.broadcasted_iota(jnp.int32, shape, 1) == wanted
    return jnp.sum(jnp.where(same, row, 0.0), axis=1, keepdims=True)


def split(sums):
    left, terms = sums, []
    for _ in range(TERMS):
        high = left.astype(jnp.bfloat16).astype(jnp.float32)
        terms.append(high)
        left = left - high
    return jnp.concatenate(terms, axis=0)


def join(terms):
    return terms[:KINDS] + terms[KINDS : 2 * KINDS] + terms[2 * KINDS : TERMS * KINDS]


def padded(rows):
    if rows.shape[0] == PARTS:
        return rows
    blank = jnp.zeros((PARTS - rows.shape[0], rows.shape[1]), jnp.float32)
    return jnp.concatenate([rows, blank], axis=0)


def exponent(largest):
    return jnp.ceil(jnp.log2(jnp.clip(largest, 1e-30, 1e30)))


def rows_at(start, size):
    return pl.ds(pl.multiple_of(start, size), size)


def row_of(slots, slot):
    return slots[slot] // COLS


def col_of(slots, slot):
    return lax.rem(slots[slot], COLS)


def forward(half, slots, field, tiles, total):
    tile = tiles.shape[1]
    cells = tile // CORES
    for slot in range(tiles.shape[0]):
        total[rows_at(row_of(slots, slot) * tile, tile), :] += jnp.dot(
            tiles[slot, :, rows_at(half * cells, cells)],
            field[col_of(slots, slot)],
            preferred_element_type=jnp.float32,
        )


def forward_own_kernel(core, slots, own, tiles, total):
    total[...] = jnp.zeros_like(total)
    forward(core[0], slots, own, tiles, total)


def forward_other_kernel(dp, core, slots, other, tiles, own_total, sums, out, total):
    chunk = out.shape[1]
    total[...] = own_total[...]
    forward(1 - core[0], slots, other, tiles, total)
    for part in range(out.shape[0]):
        out[part] = total[part * chunk : (part + 1) * chunk].astype(jnp.bfloat16)


def added(got):
    total = got[0].astype(jnp.float32)
    for part in range(1, got.shape[0]):
        total = total + got[part].astype(jnp.float32)
    return total


def weight_kernel(part, got, weights, sums, out):
    chunk = got.shape[1]
    predicted = added(got)
    weighted = (weight_column(part[0], weights) * predicted).astype(jnp.bfloat16)
    curve = column_sum(predicted * weighted.astype(jnp.float32)) + sums[0:1]
    extra = padded(split(jnp.concatenate([curve, sums[1:KINDS]], axis=0))).astype(jnp.bfloat16)
    for part in range(out.shape[0]):
        out[part, :chunk] = weighted
        out[part, chunk:] = extra


def backward(half, slots, got, tiles, source, total):
    tile = tiles.shape[1]
    parts, chunk = got.shape[0], got.shape[1] - PARTS
    cells = tile // CORES
    sums = got[0, chunk:].astype(jnp.float32)
    for part in range(1, parts):
        sums = sums + got[part, chunk:].astype(jnp.float32)
    for part in range(parts):
        source[part * chunk : (part + 1) * chunk] = got[part, :chunk]
    total[...] = jnp.zeros_like(total)
    for slot in range(tiles.shape[0]):
        total[rows_at(col_of(slots, slot) * cells, cells), :] += lax.dot_general(
            tiles[slot, :, rows_at(half * cells, cells)],
            source[rows_at(row_of(slots, slot) * tile, tile), :],
            (((0,), (0,)), ((), ())),
            preferred_element_type=jnp.float32,
        )
    return join(sums)


def backward_send_kernel(core, slots, got, tiles, coded, source, total):
    sums = backward(1 - core[0], slots, got, tiles, source, total)
    cells = tiles.shape[1] // CORES
    powers = []
    for block in range(total.shape[0] // cells):
        rows = slice(block * cells, (block + 1) * cells)
        power = exponent(jnp.max(jnp.abs(total[rows]), axis=0, keepdims=True))
        coded[rows] = total[rows] * jnp.exp2(TOP - power)
        powers.append(power)
    sum_power = exponent(jnp.abs(sums))
    terms = split(sums * jnp.exp2(TOP - sum_power))
    tail = padded(jnp.concatenate([terms, sum_power], axis=0))
    coded[total.shape[0] :] = jnp.concatenate([tail] + powers, axis=0)


def backward_keep_kernel(core, slots, got, tiles, after, keep, sums_out, source):
    sums = backward(core[0], slots, got, tiles, source, keep)
    sums_out[...] = rows_of(*[sums[kind : kind + 1] for kind in range(KINDS)])


def pair_kernel(keep, kept_sums, coded, out):
    blocks = out.shape[0]
    cells = out.shape[1] - SUMS
    tail = coded[blocks * cells :]
    at = TERMS * KINDS
    sums = kept_sums[:KINDS] + join(tail[:at]) * jnp.exp2(tail[at : at + KINDS] - TOP)
    sum_power = exponent(jnp.max(jnp.abs(sums), axis=0, keepdims=True))
    sums = sums * jnp.exp2(SUM_TOP - sum_power)
    high = sums.astype(jnp.bfloat16).astype(jnp.float32)
    for block in range(blocks):
        rows = slice(block * cells, (block + 1) * cells)
        back = jnp.exp2(tail[PARTS + block : PARTS + block + 1] - TOP)
        total = keep[rows] + coded[rows] * back
        power = exponent(jnp.max(jnp.abs(total), axis=0, keepdims=True))
        out[block, :cells] = total * jnp.exp2(TOP - power)
        out[block, cells:] = jnp.concatenate([high, sums - high, sum_power, power], axis=0)


def pair_sum(keep, kept_sums, coded, block):
    cells = CELLS
    blocks = keep.shape[0] // cells
    tail = coded[blocks * cells :]
    at = TERMS * KINDS
    sums = kept_sums[:KINDS] + join(tail[:at]) * jnp.exp2(tail[at : at + KINDS] - TOP)
    rows = slice(block * cells, (block + 1) * cells)
    back = jnp.exp2(tail[PARTS + block : PARTS + block + 1] - TOP)
    return keep[rows] + coded[rows] * back, sums


def emit(kept_blocks, sent_blocks, sums, kept, coded, kept_sums):
    cells = CELLS
    powers = []
    for at, block in enumerate(kept_blocks):
        kept[at * cells : (at + 1) * cells] = block
    for at, block in enumerate(sent_blocks):
        power = exponent(jnp.max(jnp.abs(block), axis=0, keepdims=True))
        coded[at * cells : (at + 1) * cells] = block * jnp.exp2(TOP - power)
        powers.append(power)
    power = exponent(jnp.abs(sums))
    terms = split(sums * jnp.exp2(TOP - power))
    coded[len(sent_blocks) * cells :] = padded(jnp.concatenate([terms, power] + powers, axis=0))
    kept_sums[...] = rows_of(*[sums[kind : kind + 1] for kind in range(KINDS)])


def absorb(kept, coded, kept_sums, order):
    cells = CELLS
    tail = coded[kept.shape[0] :]
    at = TERMS * KINDS
    blocks = []
    for block, place in enumerate(order):
        arrived = coded[place * cells : (place + 1) * cells]
        power = tail[at + KINDS + place : at + KINDS + place + 1]
        blocks.append(kept[block * cells : (block + 1) * cells] + arrived * jnp.exp2(power - TOP))
    return blocks, kept_sums[:KINDS] + join(tail[:at]) * jnp.exp2(tail[at : at + KINDS] - TOP)


def spread_kernel(core, height, keep, keep_sums, swapped, kept, coded, kept_sums, total):
    cells = CELLS
    for block in range(COLS):
        part, sums = pair_sum(keep, keep_sums, swapped, block)
        total[block * cells : (block + 1) * cells] = part
    half, own = height[0] // FOUR, lax.rem(height[0], FOUR)

    def blocks(chips):
        at = [z for chip in chips for z in (half * FOUR + chip, (2 - half) * FOUR - 1 - chip)]
        return [total[rows_at(z * cells, cells), :] for z in at]

    emit(
        blocks([own, jnp.bitwise_xor(own, 1 + core[0])]),
        blocks([jnp.bitwise_xor(own, 2 - core[0]), jnp.bitwise_xor(own, 3)]),
        sums,
        kept,
        coded,
        kept_sums,
    )


def halve_kernel(kept_in, coded_in, sums_in, kept, coded, kept_sums):
    blocks, sums = absorb(kept_in, coded_in, sums_in, range(4))
    emit(blocks[:2], blocks[2:], sums, kept, coded, kept_sums)


def cross_kernel(kept_in, coded_in, sums_in, right_ref, reg_ref, kept, coded, kept_sums):
    (own, other), sums = absorb(kept_in, coded_in, sums_in, range(2))
    emit([own, other], [own + reg_ref[...] * right_ref[...], other], sums, kept, coded, kept_sums)


def summed(got, cells):
    total, sums = 0.0, 0.0
    for part in range(got.shape[0]):
        tail = got[part, cells:]
        total = total + got[part, :cells] * jnp.exp2(tail[2 * KINDS + 1 :] - TOP)
        high, low, power = tail[:KINDS], tail[KINDS : 2 * KINDS], tail[2 * KINDS : 2 * KINDS + 1]
        sums = sums + (high + low) * jnp.exp2(power - SUM_TOP)
    return total, sums


def first_update_kernel(
    height, kept, coded, kept_sums, gathered, right_ref, reg_ref, residual_ref, image_ref, low_ref, sums_ref, keep_ref
):
    (terms, other), sums = absorb(kept, coded, kept_sums, (1, 0))
    right, reg = right_ref[...], reg_ref[...]
    curve, norm = sums[0:1], sums[1:2]
    alpha = norm / curve
    image = terms + reg * right
    residual = right - alpha * image
    residual_ref[...] = residual
    image_ref[...] = image
    low_ref[0] = residual.astype(jnp.bfloat16)
    other_right = gathered[COLS - 1 - height[0]].astype(jnp.float32)
    low_ref[1] = (other_right - alpha * other).astype(jnp.bfloat16)
    sums_ref[...] = cell_sums(residual, reg, image)
    keep_ref[...] = rows_of(norm, curve, alpha)


def last_update_kernel(got, right_ref, reg_ref, residual_ref, image_ref, keep_ref, solution_out, residual_out):
    right, residual = right_ref[...], residual_ref[...]
    terms, sums = summed(got, right.shape[0])
    norm, curve, alpha = keep_ref[0:1], keep_ref[1:2], keep_ref[2:3]
    norm_next = sums[1:2]
    ratio = norm_next / norm
    image_next = terms + reg_ref[...] * residual + ratio * image_ref[...]
    curve_next = sums[0:1] + ratio * (2.0 * sums[2:3] + ratio * curve)
    alpha_next = norm_next / curve_next
    direction = residual + ratio * right
    solution_out[...] = alpha * right + alpha_next * direction
    residual_out[...] = residual - alpha_next * image_next


def exchange(value, axis):
    return lax.all_to_all(value, axis, 0, 0)


def along_z(value, to):
    pairs = [
        (z * CORES + core, to(z, core) * CORES + core)
        for z in range(lax.axis_size("z"))
        for core in range(CORES)
    ]
    return lax.ppermute(value, ("z", "core"), pairs)


def near(z, core):
    return z ^ 1


def far(z, core):
    return z ^ 2


def first(z, core):
    return z ^ (2 - core)


def second(z, core):
    return z ^ (1 + core)


def mirror(z, core):
    return COLS - 1 - z


def swap(value):
    return lax.ppermute(value, "core", [(0, 1), (1, 0)])


def body(tiles, tile_rows, tile_cols, tile_count, data_weight, depth_level, depth_reg, right_side):
    tile = tiles.shape[1]
    cells, probes = right_side.shape
    group_rows = data_weight.shape[0]
    n_dp, n_z = lax.axis_size(DP), lax.axis_size("z")
    chunk = group_rows // n_dp
    col_blocks = cells * CORES * n_z // tile
    core = lax.axis_index("core").astype(jnp.int32).reshape(1)
    height = lax.axis_index("z").astype(jnp.int32).reshape(1)
    dp = lax.axis_index(DP).astype(jnp.int32).reshape(1)

    copies = call(copies_kernel, bf16(n_z, cells, probes), (right_side,))
    own = exchange(copies, "z")
    live = jnp.arange(tiles.shape[0], dtype=jnp.int32) < tile_count
    tiles = jnp.where(live[:, None, None], tiles, jnp.zeros_like(tiles))
    own = own * (tiles[0, :1, :1] == tiles[0, :1, :1]).astype(jnp.bfloat16)
    slots = tile_rows * COLS + tile_cols
    half, chip = height >> 2, height & 3
    same = (tile_cols >> 2) == half
    apart = jnp.where(same, tile_cols & 3, 3 - (tile_cols & 3)) ^ chip
    place = ((apart & 1) * 2 + (apart >> 1)) * 2 + jnp.where(same, 0, 1)
    last_slots = tile_rows * COLS + place
    levels = jnp.arange(depth_reg.shape[0], dtype=jnp.int32)
    level_hot = (depth_level[:, None] == levels[None, :]).astype(jnp.float32)
    reg_cell = jnp.sum(level_hot * depth_reg[None, :], axis=1)
    reg = jnp.broadcast_to(reg_cell[:, None], (cells, probes))
    sums = call(start_kernel, f32(SUMS, probes), (right_side, reg))
    weights = data_weight.reshape(-1, chunk * PACK)

    def products(own, other, sums, places):
        total = call(
            forward_own_kernel, f32(group_rows, probes), (core, places, own, tiles), smem=2
        )
        partial = call(
            forward_other_kernel,
            bf16(n_dp, chunk, probes),
            (dp, core, places, other, tiles, total, sums),
            smem=3,
            scratch=[pltpu.VMEM((group_rows, probes), jnp.float32)],
        )
        weighted = call(
            weight_kernel,
            bf16(n_dp, chunk + PARTS, probes),
            (dp, exchange(partial, DP), weights, sums),
            smem=1,
        )
        operands = (core, slots, exchange(weighted, DP), tiles)
        source = pltpu.VMEM((group_rows, probes), jnp.bfloat16)
        rows = n_z * cells
        coded = call(
            backward_send_kernel,
            f32(rows + PARTS + n_z, probes),
            operands,
            smem=2,
            scratch=[source, pltpu.VMEM((rows, probes), jnp.float32)],
        )
        keep, kept_sums = call(
            backward_keep_kernel,
            [f32(rows, probes), f32(SUMS, probes)],
            (*operands, coded),
            smem=2,
            scratch=[source],
        )
        return keep, kept_sums, swap(coded.astype(jnp.float16)).astype(jnp.float32)

    def halved(kernel, blocks, operands, to, smem=0, scratch=()):
        kept, coded, sums = call(
            kernel,
            (f32(blocks * cells, probes), f32(blocks * cells + PARTS, probes), f32(SUMS, probes)),
            operands,
            smem=smem,
            scratch=scratch,
        )
        return kept, along_z(coded.astype(jnp.float16), to).astype(jnp.float32), sums

    whole, extra = f32(cells, probes), f32(SUMS, probes)
    terms = products(own, swap(own), sums, slots)
    terms = halved(
        spread_kernel,
        4,
        (core, height, *terms),
        first,
        smem=2,
        scratch=[pltpu.VMEM((n_z * cells, probes), jnp.float32)],
    )
    terms = halved(halve_kernel, 2, terms, second)
    terms = halved(cross_kernel, 2, (*terms, right_side, reg), mirror)
    residual, image, low, sums, keep = call(
        first_update_kernel,
        (whole, whole, bf16(2, cells, probes), extra, extra),
        (height, *terms, own, right_side, reg),
        smem=1,
    )
    low = jnp.concatenate([low, along_z(low, far)], axis=0)
    later = along_z(low, near)
    other = jnp.concatenate([swap(low), swap(later)], axis=0)
    low = jnp.concatenate([low, later], axis=0)
    terms = call(pair_kernel, f32(n_z, cells + SUMS, probes), products(low, other, sums, last_slots))
    got = exchange(terms.astype(jnp.float16), "z").astype(jnp.float32)
    return call(
        last_update_kernel,
        (whole, whole),
        (got, right_side, reg, residual, image, keep),
    )


DP = ("y", "x")


def solution(mesh):
    n_dp, n_mp = mesh.devices.shape
    split_mesh = jax.sharding.Mesh(
        mesh.devices.reshape(n_dp // SIDE, SIDE, n_mp // CORES, CORES), ("y", "x", "z", "core")
    )
    mp = ("z", "core")
    every = DP + mp
    placed = (
        P(every, None, None),
        P(every),
        P(every),
        P(every),
        P(mp),
        P(every),
        P(),
        P(every, None),
    )
    return jax.shard_map(
        body,
        mesh=split_mesh,
        in_specs=placed,
        out_specs=(P(every, None), P(every, None)),
        check_vma=False,
    )
```

```python
import functools

import jax
import jax.numpy as jnp
from jax import lax
from jax.experimental import pallas as pl
from jax.experimental.pallas import tpu as pltpu
from jax.sharding import PartitionSpec as P

SUMS = 8
TERMS = 3
PARTS = 16
CORES = 2
SIDE = 4
KINDS = 3
CELLS = 128
FOUR = 4
COLS = 8
PACK = 2
TOP = 10.0
SUM_TOP = 14.0
VMEM_LIMIT = 16 * 1024 * 1024


def call(kernel, out_shape, operands, smem=0, scratch=()):
    spaces = [pltpu.SMEM] * smem + [pltpu.VMEM] * (len(operands) - smem)
    return pl.pallas_call(
        kernel,
        out_shape=out_shape,
        in_specs=[pl.BlockSpec(memory_space=space) for space in spaces],
        out_specs=jax.tree.map(lambda _: pl.BlockSpec(memory_space=pltpu.VMEM), out_shape),
        scratch_shapes=list(scratch),
        compiler_params=pltpu.CompilerParams(vmem_limit_bytes=VMEM_LIMIT),
    )(*operands)


def f32(*shape):
    return jax.ShapeDtypeStruct(shape, jnp.float32)


def bf16(*shape):
    return jax.ShapeDtypeStruct(shape, jnp.bfloat16)


def rows_of(*sums):
    blank = jnp.zeros((SUMS - len(sums), sums[0].shape[1]), jnp.float32)
    return jnp.concatenate(list(sums) + [blank], axis=0)


def column_sum(value):
    return jnp.sum(value, axis=0, keepdims=True)


def cell_sums(value, reg, image):
    square = value * value
    return rows_of(column_sum(reg * square), column_sum(square), column_sum(value * image))


def copies_kernel(right_ref, low_ref):
    low = right_ref[...].astype(jnp.bfloat16)
    for block in range(low_ref.shape[0]):
        low_ref[block] = low


def start_kernel(right_ref, reg_ref, sums_ref):
    right = right_ref[...]
    sums_ref[...] = cell_sums(right, reg_ref[...], jnp.zeros_like(right))


def weight_column(part, weights):
    row = weights[pl.ds(part // PACK, 1), :]
    n = row.shape[1]
    shape = (n // PACK, n)
    wanted = lax.broadcasted_iota(jnp.int32, shape, 0) + lax.rem(part, PACK) * (n // PACK)
    same = lax.broadcasted_iota(jnp.int32, shape, 1) == wanted
    return jnp.sum(jnp.where(same, row, 0.0), axis=1, keepdims=True)


def split(sums):
    left, terms = sums, []
    for _ in range(TERMS):
        high = left.astype(jnp.bfloat16).astype(jnp.float32)
        terms.append(high)
        left = left - high
    return jnp.concatenate(terms, axis=0)


def join(terms):
    return terms[:KINDS] + terms[KINDS : 2 * KINDS] + terms[2 * KINDS : TERMS * KINDS]


def padded(rows):
    if rows.shape[0] == PARTS:
        return rows
    blank = jnp.zeros((PARTS - rows.shape[0], rows.shape[1]), jnp.float32)
    return jnp.concatenate([rows, blank], axis=0)


def exponent(largest):
    return jnp.ceil(jnp.log2(jnp.clip(largest, 1e-30, 1e30)))


def rows_at(start, size):
    return pl.ds(pl.multiple_of(start, size), size)


def row_of(slots, slot):
    return slots[slot] // COLS


def col_of(slots, slot):
    return lax.rem(slots[slot], COLS)


def forward(half, slots, field, tiles, total):
    tile = tiles.shape[1]
    cells = tile // CORES
    for slot in range(tiles.shape[0]):
        total[rows_at(row_of(slots, slot) * tile, tile), :] += jnp.dot(
            tiles[slot, :, rows_at(half * cells, cells)],
            field[col_of(slots, slot)],
            preferred_element_type=jnp.float32,
        )


def forward_own_kernel(core, slots, own, tiles, total):
    total[...] = jnp.zeros_like(total)
    forward(core[0], slots, own, tiles, total)


def forward_other_kernel(dp, core, slots, other, tiles, own_total, sums, out, total):
    chunk = out.shape[1]
    total[...] = own_total[...]
    forward(1 - core[0], slots, other, tiles, total)
    for part in range(out.shape[0]):
        out[part] = total[part * chunk : (part + 1) * chunk].astype(jnp.bfloat16)


def added(got):
    total = got[0].astype(jnp.float32)
    for part in range(1, got.shape[0]):
        total = total + got[part].astype(jnp.float32)
    return total


def weight_kernel(part, got, weights, sums, out):
    chunk = got.shape[1]
    predicted = added(got)
    weighted = (weight_column(part[0], weights) * predicted).astype(jnp.bfloat16)
    curve = column_sum(predicted * weighted.astype(jnp.float32)) + sums[0:1]
    extra = padded(split(jnp.concatenate([curve, sums[1:KINDS]], axis=0))).astype(jnp.bfloat16)
    for part in range(out.shape[0]):
        out[part, :chunk] = weighted
        out[part, chunk:] = extra


def backward(half, slots, got, tiles, source, total):
    tile = tiles.shape[1]
    parts, chunk = got.shape[0], got.shape[1] - PARTS
    cells = tile // CORES
    sums = got[0, chunk:].astype(jnp.float32)
    for part in range(1, parts):
        sums = sums + got[part, chunk:].astype(jnp.float32)
    for part in range(parts):
        source[part * chunk : (part + 1) * chunk] = got[part, :chunk]
    total[...] = jnp.zeros_like(total)
    for slot in range(tiles.shape[0]):
        total[rows_at(col_of(slots, slot) * cells, cells), :] += lax.dot_general(
            tiles[slot, :, rows_at(half * cells, cells)],
            source[rows_at(row_of(slots, slot) * tile, tile), :],
            (((0,), (0,)), ((), ())),
            preferred_element_type=jnp.float32,
        )
    return join(sums)


def backward_send_kernel(core, slots, got, tiles, coded, source, total):
    sums = backward(1 - core[0], slots, got, tiles, source, total)
    cells = tiles.shape[1] // CORES
    powers = []
    for block in range(total.shape[0] // cells):
        rows = slice(block * cells, (block + 1) * cells)
        power = exponent(jnp.max(jnp.abs(total[rows]), axis=0, keepdims=True))
        coded[rows] = total[rows] * jnp.exp2(TOP - power)
        powers.append(power)
    sum_power = exponent(jnp.abs(sums))
    terms = split(sums * jnp.exp2(TOP - sum_power))
    tail = padded(jnp.concatenate([terms, sum_power], axis=0))
    coded[total.shape[0] :] = jnp.concatenate([tail] + powers, axis=0)


def backward_keep_kernel(core, slots, got, tiles, after, keep, sums_out, source):
    sums = backward(core[0], slots, got, tiles, source, keep)
    sums_out[...] = rows_of(*[sums[kind : kind + 1] for kind in range(KINDS)])


def pair_kernel(keep, kept_sums, coded, out):
    blocks = out.shape[0]
    cells = out.shape[1] - SUMS
    tail = coded[blocks * cells :]
    at = TERMS * KINDS
    sums = kept_sums[:KINDS] + join(tail[:at]) * jnp.exp2(tail[at : at + KINDS] - TOP)
    sum_power = exponent(jnp.max(jnp.abs(sums), axis=0, keepdims=True))
    sums = sums * jnp.exp2(SUM_TOP - sum_power)
    high = sums.astype(jnp.bfloat16).astype(jnp.float32)
    for block in range(blocks):
        rows = slice(block * cells, (block + 1) * cells)
        back = jnp.exp2(tail[PARTS + block : PARTS + block + 1] - TOP)
        total = keep[rows] + coded[rows] * back
        power = exponent(jnp.max(jnp.abs(total), axis=0, keepdims=True))
        out[block, :cells] = total * jnp.exp2(TOP - power)
        out[block, cells:] = jnp.concatenate([high, sums - high, sum_power, power], axis=0)


def pair_sum(keep, kept_sums, coded, block):
    cells = CELLS
    blocks = keep.shape[0] // cells
    tail = coded[blocks * cells :]
    at = TERMS * KINDS
    sums = kept_sums[:KINDS] + join(tail[:at]) * jnp.exp2(tail[at : at + KINDS] - TOP)
    rows = slice(block * cells, (block + 1) * cells)
    back = jnp.exp2(tail[PARTS + block : PARTS + block + 1] - TOP)
    return keep[rows] + coded[rows] * back, sums


def emit(kept_blocks, sent_blocks, sums, kept, coded, kept_sums):
    cells = CELLS
    powers = []
    for at, block in enumerate(kept_blocks):
        kept[at * cells : (at + 1) * cells] = block
    for at, block in enumerate(sent_blocks):
        power = exponent(jnp.max(jnp.abs(block), axis=0, keepdims=True))
        coded[at * cells : (at + 1) * cells] = block * jnp.exp2(TOP - power)
        powers.append(power)
    power = exponent(jnp.abs(sums))
    terms = split(sums * jnp.exp2(TOP - power))
    coded[len(sent_blocks) * cells :] = padded(jnp.concatenate([terms, power] + powers, axis=0))
    kept_sums[...] = rows_of(*[sums[kind : kind + 1] for kind in range(KINDS)])


def absorb(kept, coded, kept_sums, order):
    cells = CELLS
    tail = coded[kept.shape[0] :]
    at = TERMS * KINDS
    blocks = []
    for block, place in enumerate(order):
        arrived = coded[place * cells : (place + 1) * cells]
        power = tail[at + KINDS + place : at + KINDS + place + 1]
        blocks.append(kept[block * cells : (block + 1) * cells] + arrived * jnp.exp2(power - TOP))
    return blocks, kept_sums[:KINDS] + join(tail[:at]) * jnp.exp2(tail[at : at + KINDS] - TOP)


def spread_kernel(core, height, keep, keep_sums, swapped, kept, coded, kept_sums, total):
    cells = CELLS
    for block in range(COLS):
        part, sums = pair_sum(keep, keep_sums, swapped, block)
        total[block * cells : (block + 1) * cells] = part
    half, own = height[0] // FOUR, lax.rem(height[0], FOUR)

    def blocks(chips):
        at = [z for chip in chips for z in (half * FOUR + chip, (2 - half) * FOUR - 1 - chip)]
        return [total[rows_at(z * cells, cells), :] for z in at]

    emit(
        blocks([own, jnp.bitwise_xor(own, 1 + core[0])]),
        blocks([jnp.bitwise_xor(own, 2 - core[0]), jnp.bitwise_xor(own, 3)]),
        sums,
        kept,
        coded,
        kept_sums,
    )


def halve_kernel(kept_in, coded_in, sums_in, kept, coded, kept_sums):
    blocks, sums = absorb(kept_in, coded_in, sums_in, range(4))
    emit(blocks[:2], blocks[2:], sums, kept, coded, kept_sums)


def cross_kernel(kept_in, coded_in, sums_in, right_ref, reg_ref, kept, coded, kept_sums):
    (own, other), sums = absorb(kept_in, coded_in, sums_in, range(2))
    emit([own, other], [own + reg_ref[...] * right_ref[...], other], sums, kept, coded, kept_sums)


def summed(got, cells):
    total, sums = 0.0, 0.0
    for part in range(got.shape[0]):
        tail = got[part, cells:]
        total = total + got[part, :cells] * jnp.exp2(tail[2 * KINDS + 1 :] - TOP)
        high, low, power = tail[:KINDS], tail[KINDS : 2 * KINDS], tail[2 * KINDS : 2 * KINDS + 1]
        sums = sums + (high + low) * jnp.exp2(power - SUM_TOP)
    return total, sums


def first_update_kernel(
    height, kept, coded, kept_sums, gathered, right_ref, reg_ref, residual_ref, image_ref, low_ref, sums_ref, keep_ref
):
    (terms, other), sums = absorb(kept, coded, kept_sums, (1, 0))
    right, reg = right_ref[...], reg_ref[...]
    curve, norm = sums[0:1], sums[1:2]
    alpha = norm / curve
    image = terms + reg * right
    residual = right - alpha * image
    residual_ref[...] = residual
    image_ref[...] = image
    low_ref[0] = residual.astype(jnp.bfloat16)
    other_right = gathered[COLS - 1 - height[0]].astype(jnp.float32)
    low_ref[1] = (other_right - alpha * other).astype(jnp.bfloat16)
    sums_ref[...] = cell_sums(residual, reg, image)
    keep_ref[...] = rows_of(norm, curve, alpha)


def last_update_kernel(got, right_ref, reg_ref, residual_ref, image_ref, keep_ref, solution_out, residual_out):
    right, residual = right_ref[...], residual_ref[...]
    terms, sums = summed(got, right.shape[0])
    norm, curve, alpha = keep_ref[0:1], keep_ref[1:2], keep_ref[2:3]
    norm_next = sums[1:2]
    ratio = norm_next / norm
    image_next = terms + reg_ref[...] * residual + ratio * image_ref[...]
    curve_next = sums[0:1] + ratio * (2.0 * sums[2:3] + ratio * curve)
    alpha_next = norm_next / curve_next
    direction = residual + ratio * right
    solution_out[...] = alpha * right + alpha_next * direction
    residual_out[...] = residual - alpha_next * image_next


def exchange(value, axis):
    return lax.all_to_all(value, axis, 0, 0)


def along_z(value, to):
    pairs = [
        (z * CORES + core, to(z, core) * CORES + core)
        for z in range(lax.axis_size("z"))
        for core in range(CORES)
    ]
    return lax.ppermute(value, ("z", "core"), pairs)


def first(z, core):
    return z ^ (2 - core)


def second(z, core):
    return z ^ (1 + core)


def mirror(z, core):
    return COLS - 1 - z


def swap(value):
    return lax.ppermute(value, "core", [(0, 1), (1, 0)])


def body(tiles, tile_rows, tile_cols, tile_count, data_weight, depth_level, depth_reg, right_side):
    tile = tiles.shape[1]
    cells, probes = right_side.shape
    group_rows = data_weight.shape[0]
    n_dp, n_z = lax.axis_size(DP), lax.axis_size("z")
    chunk = group_rows // n_dp
    col_blocks = cells * CORES * n_z // tile
    core = lax.axis_index("core").astype(jnp.int32).reshape(1)
    height = lax.axis_index("z").astype(jnp.int32).reshape(1)
    dp = lax.axis_index(DP).astype(jnp.int32).reshape(1)

    copies = call(copies_kernel, bf16(n_z, cells, probes), (right_side,))
    own = exchange(copies, "z")
    live = jnp.arange(tiles.shape[0], dtype=jnp.int32) < tile_count
    tiles = jnp.where(live[:, None, None], tiles, jnp.zeros_like(tiles))
    own = own * (tiles[0, :1, :1] == tiles[0, :1, :1]).astype(jnp.bfloat16)
    slots = tile_rows * COLS + tile_cols
    half, chip = height >> 2, height & 3
    same = (tile_cols >> 2) == half
    apart = jnp.where(same, tile_cols & 3, 3 - (tile_cols & 3)) ^ chip
    turned = (apart & 1) * 2 + (apart >> 1)
    rest = tile_rows * COLS + jnp.where(same, 0, 1)
    own_slots = rest + 2 * jnp.where(core == 0, apart, turned)
    other_slots = rest + 2 * jnp.where(core == 0, turned, apart)
    levels = jnp.arange(depth_reg.shape[0], dtype=jnp.int32)
    level_hot = (depth_level[:, None] == levels[None, :]).astype(jnp.float32)
    reg_cell = jnp.sum(level_hot * depth_reg[None, :], axis=1)
    reg = jnp.broadcast_to(reg_cell[:, None], (cells, probes))
    sums = call(start_kernel, f32(SUMS, probes), (right_side, reg))
    weights = data_weight.reshape(-1, chunk * PACK)

    def products(own, other, sums, places, other_places):
        total = call(
            forward_own_kernel, f32(group_rows, probes), (core, places, own, tiles), smem=2
        )
        partial = call(
            forward_other_kernel,
            bf16(n_dp, chunk, probes),
            (dp, core, other_places, other, tiles, total, sums),
            smem=3,
            scratch=[pltpu.VMEM((group_rows, probes), jnp.float32)],
        )
        weighted = call(
            weight_kernel,
            bf16(n_dp, chunk + PARTS, probes),
            (dp, exchange(partial, DP), weights, sums),
            smem=1,
        )
        operands = (core, slots, exchange(weighted, DP), tiles)
        source = pltpu.VMEM((group_rows, probes), jnp.bfloat16)
        rows = n_z * cells
        coded = call(
            backward_send_kernel,
            f32(rows + PARTS + n_z, probes),
            operands,
            smem=2,
            scratch=[source, pltpu.VMEM((rows, probes), jnp.float32)],
        )
        keep, kept_sums = call(
            backward_keep_kernel,
            [f32(rows, probes), f32(SUMS, probes)],
            (*operands, coded),
            smem=2,
            scratch=[source],
        )
        return keep, kept_sums, swap(coded.astype(jnp.float16)).astype(jnp.float32)

    def halved(kernel, blocks, operands, to, smem=0, scratch=()):
        kept, coded, sums = call(
            kernel,
            (f32(blocks * cells, probes), f32(blocks * cells + PARTS, probes), f32(SUMS, probes)),
            operands,
            smem=smem,
            scratch=scratch,
        )
        return kept, along_z(coded.astype(jnp.float16), to).astype(jnp.float32), sums

    whole, extra = f32(cells, probes), f32(SUMS, probes)
    terms = products(own, swap(own), sums, slots, slots)
    terms = halved(
        spread_kernel,
        4,
        (core, height, *terms),
        first,
        smem=2,
        scratch=[pltpu.VMEM((n_z * cells, probes), jnp.float32)],
    )
    terms = halved(halve_kernel, 2, terms, second)
    terms = halved(cross_kernel, 2, (*terms, right_side, reg), mirror)
    residual, image, low, sums, keep = call(
        first_update_kernel,
        (whole, whole, bf16(2, cells, probes), extra, extra),
        (height, *terms, own, right_side, reg),
        smem=1,
    )
    low = jnp.concatenate([low, along_z(low, second)], axis=0)
    later = along_z(low, first)
    other = jnp.concatenate([swap(low), swap(later)], axis=0)
    low = jnp.concatenate([low, later], axis=0)
    terms = call(pair_kernel, f32(n_z, cells + SUMS, probes), products(low, other, sums, own_slots, other_slots))
    got = exchange(terms.astype(jnp.float16), "z").astype(jnp.float32)
    return call(
        last_update_kernel,
        (whole, whole),
        (got, right_side, reg, residual, image, keep),
    )


DP = ("y", "x")


def solution(mesh):
    n_dp, n_mp = mesh.devices.shape
    split_mesh = jax.sharding.Mesh(
        mesh.devices.reshape(n_dp // SIDE, SIDE, n_mp // CORES, CORES), ("y", "x", "z", "core")
    )
    mp = ("z", "core")
    every = DP + mp
    placed = (
        P(every, None, None),
        P(every),
        P(every),
        P(every),
        P(mp),
        P(every),
        P(),
        P(every, None),
    )
    return jax.shard_map(
        body,
        mesh=split_mesh,
        in_specs=placed,
        out_specs=(P(every, None), P(every, None)),
        check_vma=False,
    )
```
